32 devices in a mesh: ctx: 4 (over x, core), mp: 8 (over z, y).
Axes of the slice: x: 2, y: 2, z: 4, core: 2. Of those that a mesh axis runs over, the one named last changes fastest.
Arguments:
- queries: bfloat16 [4096, 4096], P('ctx', 'mp'), may hold values from -320 to 320
- keys_values: bfloat16 [4096, 2048], P('ctx', 'mp'), may hold values from -40 to 40
- query_taps: float32 [4, 4096], P(None, 'mp'), may hold values from -2.5 to 2.5
- pair_taps: float32 [4, 2048], P(None, 'mp'), may hold values from -2.5 to 2.5
- out_gain: float32 [4096], P('mp'), may hold values from 0.1 to 1.9
Outputs:
- head_outputs: bfloat16 [4096, 4096], P('ctx', 'mp')
The draws below stay inside these ranges and needn't reach their ends.
All inputs are finite; a program needn't handle non-finite values.
Results may differ from the reference program's by a relative error of at most 0.012.
The reference program's roundings to bfloat16 on the way count: a program that leaves them out, or rounds other values in their place, can miss the bound.
Values may be sent and summed in bfloat16 or wider, within the bound.
A program may use at most 64 MiB of HBM per device.

```python
import math
import jax
import jax.numpy as jnp
import numpy as np
from jax import lax

HEADS = 32
KV_HEADS = 8
HEAD_CHANNELS = 128
TAPS = 4
TRANSFORM_BLOCK = 128
KEEP = 16
FOLDED_SPAN = 512
SEQ = 4096
N_CTX = 4


def draw_queries(key, part):
    base = jnp.clip(jax.random.normal(key, (SEQ, HEADS * HEAD_CHANNELS), jnp.float32), -4.0, 4.0)
    return base.astype(jnp.bfloat16)


def draw_keys_values(key, part):
    columns = 2 * KV_HEADS * HEAD_CHANNELS
    is_value = jnp.arange(columns) // HEAD_CHANNELS % 2 == 1
    channel_draw = jax.random.uniform(jax.random.fold_in(key, 21), (columns,), jnp.float32)
    lower = math.log(0.5)
    upper = jnp.where(is_value, math.log(5.0), math.log(1.5))
    channel_scale = jnp.exp(lower + (upper - lower) * channel_draw)
    row_scale = jnp.exp(jax.random.uniform(jax.random.fold_in(key, 22), (SEQ, 1), jnp.float32, math.log(0.7), math.log(2.0)))
    base = jnp.clip(jax.random.normal(jax.random.fold_in(key, 25), (SEQ, columns), jnp.float32), -4.0, 4.0)
    return (base * channel_scale * row_scale).astype(jnp.bfloat16)


def steps_of(own_key, shape, split, smallest, largest):
    gain = 1.0
    for position, shards_of in split:
        draws = jax.random.uniform(jax.random.fold_in(jax.random.fold_in(own_key, 6), position), (shards_of,), jnp.float32, smallest / len(split), largest / len(split))
        gain = gain * jnp.repeat(jnp.exp(draws), shape[position] // shards_of).reshape((-1,) + (1,) * (len(shape) - 1 - position))
    return gain


def scatter_about(stream_key, shape, spread, most, shards=(), kind=jnp.bfloat16):
    loudness = steps_of(stream_key, shape, shards, -0.22, 0.18) if shards else 1.0
    values = jax.random.normal(stream_key, shape, jnp.float32) * spread * loudness
    return jnp.minimum(jnp.maximum(values, -most), most).astype(kind)


def setup_inputs(seed: int = 0) -> dict:
    key_list = jax.random.split(jax.random.key(seed), 6)
    return {
        "queries": draw_queries(jax.random.fold_in(key_list[5], 71), 0),
        "keys_values": draw_keys_values(jax.random.fold_in(key_list[5], 71), 0),
        "query_taps": scatter_about(key_list[2], (TAPS, HEADS * HEAD_CHANNELS), 0.5, 2.5, ((1, 8),), jnp.float32),
        "pair_taps": scatter_about(key_list[3], (TAPS, 2 * KV_HEADS * HEAD_CHANNELS), 0.5, 2.5, ((1, 8),), jnp.float32),
        "out_gain": jnp.clip(1.0 + 0.18 * jax.random.normal(key_list[4], (HEADS * HEAD_CHANNELS,), jnp.float32), 0.1, 1.9),
    }


def span_sources():
    sources = []
    for stored in range(2 * N_CTX):
        holder = stored // 2
        sources.append(holder if stored % 2 == 0 else 2 * N_CTX - 1 - holder)
    return np.array(sources)

def to_sequence(array):
    spans = array.reshape((2 * N_CTX, FOLDED_SPAN) + array.shape[1:])
    return spans[np.argsort(span_sources())].reshape(array.shape)

def to_storage(array):
    spans = array.reshape((2 * N_CTX, FOLDED_SPAN) + array.shape[1:])
    return spans[span_sources()].reshape(array.shape)

def rounded_values(values):
    return lax.optimization_barrier(values.astype(jnp.bfloat16)).astype(jnp.float32)

def dct_table():
    frequency = jnp.arange(KEEP, dtype=jnp.float32)[:, None]
    offset = jnp.arange(TRANSFORM_BLOCK, dtype=jnp.float32)[None, :]
    table = jnp.cos(math.pi * (offset + 0.5) * frequency / TRANSFORM_BLOCK) * math.sqrt(2.0 / TRANSFORM_BLOCK)
    table = jnp.where(frequency == 0.0, table * math.sqrt(0.5), table)
    return table.astype(jnp.bfloat16)

def causal_conv(values, weights):
    length = values.shape[0]
    lead = TAPS - 1
    padded = jnp.pad(values.astype(jnp.float32), ((lead, 0), (0, 0)))
    total = weights[0] * padded[lead:lead + length]
    for shift in range(1, TAPS):
        total = total + weights[shift] * padded[lead - shift:lead - shift + length]
    return total.astype(jnp.bfloat16)

def compress(values):
    blocks = values.reshape(values.shape[0] // TRANSFORM_BLOCK, TRANSFORM_BLOCK, values.shape[1]).astype(jnp.float32)
    packed = jnp.einsum('jt,btc->bjc', dct_table().astype(jnp.float32), blocks, precision=lax.Precision.HIGHEST)
    return packed.astype(jnp.bfloat16).reshape(-1, values.shape[1])

def reference(queries, keys_values, query_taps, pair_taps, out_gain):
    query_group = HEADS // KV_HEADS
    score_scale = 1.0 / math.sqrt(HEAD_CHANNELS)
    seq_queries = causal_conv(to_sequence(queries), query_taps)
    seq_pairs = causal_conv(to_sequence(keys_values), pair_taps)
    packed = compress(seq_pairs)
    query_heads = seq_queries.reshape(SEQ, KV_HEADS, query_group, HEAD_CHANNELS).transpose(1, 0, 2, 3)
    pair_heads = seq_pairs.reshape(SEQ, KV_HEADS, 2 * HEAD_CHANNELS).transpose(1, 0, 2)
    packed_heads = packed.reshape(-1, KV_HEADS, 2 * HEAD_CHANNELS).transpose(1, 0, 2)

    def head_group(operands):
        query_all, pair_all, packed_all = operands
        outputs = []
        quarter = SEQ // 4
        for portion in range(4):
            limit = (portion + 1) * quarter * KEEP // TRANSFORM_BLOCK
            seen_keys = packed_all[:limit].astype(jnp.float32)
            key_blocks = (jnp.arange(limit) // KEEP).astype(jnp.int32)

            def span_fn(pieces):
                query_span, pair_span, start = pieces
                positions = start + jnp.arange(FOLDED_SPAN).astype(jnp.int32)
                query_blocks = positions // TRANSFORM_BLOCK
                query_single_float = query_span.astype(jnp.float32)
                far = jnp.einsum('qgd,kd->qgk', query_single_float, seen_keys[:, :HEAD_CHANNELS]) * score_scale
                far = jnp.where(key_blocks[None, None, :] < query_blocks[:, None, None], far, -jnp.inf)
                entry_count = FOLDED_SPAN // TRANSFORM_BLOCK
                pair_single_float = pair_span.astype(jnp.float32)
                nearby_scores = jnp.einsum('cehp,cyp->cehy', query_single_float.reshape(entry_count, TRANSFORM_BLOCK, query_group, HEAD_CHANNELS), pair_single_float[:, :HEAD_CHANNELS].reshape(entry_count, TRANSFORM_BLOCK, HEAD_CHANNELS)) * score_scale
                causal = jnp.arange(TRANSFORM_BLOCK)[:, None, None] >= jnp.arange(TRANSFORM_BLOCK)[None, None, :]
                nearby_scores = jnp.where(causal, nearby_scores, -jnp.inf).reshape(FOLDED_SPAN, query_group, TRANSFORM_BLOCK)
                top = jnp.maximum(lax.optimization_barrier(jnp.max(far, -1)), lax.optimization_barrier(jnp.max(nearby_scores, -1)))
                far_weights = jnp.exp(far - top[..., None])
                nearby_weights = jnp.exp(nearby_scores - top[..., None])
                total = lax.optimization_barrier(jnp.sum(far_weights, -1)) + lax.optimization_barrier(jnp.sum(nearby_weights, -1))
                far_out = jnp.einsum('qgk,kd->qgd', rounded_values(far_weights), seen_keys[:, HEAD_CHANNELS:])
                nearby_output = jnp.einsum('oris,osz->oriz', rounded_values(nearby_weights).reshape(entry_count, TRANSFORM_BLOCK, query_group, TRANSFORM_BLOCK), pair_single_float[:, HEAD_CHANNELS:].reshape(entry_count, TRANSFORM_BLOCK, HEAD_CHANNELS)).reshape(FOLDED_SPAN, query_group, HEAD_CHANNELS)
                attended = (far_out + nearby_output) / total[..., None]
                return attended * lax.rsqrt(lax.optimization_barrier(jnp.mean(attended * attended, -1, keepdims=True)) + 1e-06)
            query_part = query_all[portion * quarter:(portion + 1) * quarter].reshape(quarter // FOLDED_SPAN, FOLDED_SPAN, query_group, HEAD_CHANNELS)
            pair_part = pair_all[portion * quarter:(portion + 1) * quarter].reshape(quarter // FOLDED_SPAN, FOLDED_SPAN, 2 * HEAD_CHANNELS)
            starts = (portion * quarter + FOLDED_SPAN * jnp.arange(quarter // FOLDED_SPAN)).astype(jnp.int32)
            outputs.append(lax.map(span_fn, (query_part, pair_part, starts)).reshape(quarter, query_group, HEAD_CHANNELS))
        return jnp.concatenate(outputs, 0)
    attended = lax.map(head_group, (query_heads, pair_heads, packed_heads))
    normed = attended.transpose(1, 0, 2, 3).reshape(SEQ, HEADS * HEAD_CHANNELS)
    return to_storage((normed * out_gain).astype(jnp.bfloat16))
```

```python
import functools
import math

import jax
import jax.numpy as jnp
import numpy as np
from jax import lax
from jax.experimental import pallas as pl
from jax.experimental.pallas import tpu as pltpu
from jax.sharding import PartitionSpec as P

HEAD_CHANNELS = 128
TAPS = 4
TRANSFORM_BLOCK = 128
KEEP = 16
HALO = 16

NEGATIVE = -1e30
EPSILON = 1e-06
MESH = pl.DeviceIdType.MESH


def dct_table():
    frequency = np.arange(KEEP, dtype=np.float32)[:, None]
    offset = np.arange(TRANSFORM_BLOCK, dtype=np.float32)[None, :]
    angle = np.float32(math.pi) * (offset + np.float32(0.5)) * frequency
    table = np.cos(angle / np.float32(TRANSFORM_BLOCK)) * np.float32(
        math.sqrt(2.0 / TRANSFORM_BLOCK)
    )
    table = np.where(frequency == 0.0, table * np.float32(math.sqrt(0.5)), table)
    return table.astype(jnp.bfloat16)


def nt_dot(left, right):
    return lax.dot_general(
        left, right, (((1,), (1,)), ((), ())), preferred_element_type=jnp.float32
    )


def kernel(
    shards,
    per_span,
    heads,
    q_hbm,
    kv_hbm,
    qt_hbm,
    pt_hbm,
    gain_hbm,
    table_hbm,
    out_hbm,
    xq,
    xkv,
    qt,
    pt,
    gain,
    table,
    qc,
    kvc,
    gath,
    out,
    in_sem,
    small_sem,
    own_halo_sem,
    halo_send,
    halo_recv,
    lower_send,
    upper_send,
    gath_recv,
    out_sem,
):
    place = lax.axis_index("ctx")
    block = TRANSFORM_BLOCK
    span_rows = per_span * block
    half = per_span * KEEP
    channels = HEAD_CHANNELS

    loads = {}
    for s in range(2):
        loads["kv", s] = pltpu.make_async_copy(
            kv_hbm.at[pl.ds(s * span_rows, span_rows), :],
            xkv.at[s, pl.ds(HALO, span_rows), :],
            in_sem.at[s],
        )
        loads["q", s] = pltpu.make_async_copy(
            q_hbm.at[pl.ds(s * span_rows, span_rows), :],
            xq.at[s, pl.ds(HALO, span_rows), :],
            in_sem.at[2 + s],
        )
    small = [
        pltpu.make_async_copy(source, target, small_sem.at[n])
        for n, (source, target) in enumerate(
            [(pt_hbm, pt), (table_hbm, table), (qt_hbm, qt), (gain_hbm, gain)]
        )
    ]
    loads["kv", 0].start()
    loads["kv", 1].start()
    for copy in small:
        copy.start()
    loads["q", 0].start()
    loads["q", 1].start()

    barrier = pltpu.get_barrier_semaphore()
    for d in range(1, shards):
        pl.semaphore_signal(
            barrier,
            inc=1,
            device_id={"ctx": lax.rem(place + d, shards)},
            device_id_type=MESH,
        )
    pl.semaphore_wait(barrier, shards - 1)

    def halo_copy(n, s, step):
        source, target = ((kv_hbm, xkv), (q_hbm, xq))[n]
        return pltpu.make_async_remote_copy(
            src_ref=source.at[pl.ds((s + 1) * span_rows - HALO, HALO), :],
            dst_ref=target.at[s, pl.ds(0, HALO), :],
            send_sem=halo_send.at[n, s],
            recv_sem=halo_recv.at[n, s],
            device_id={"ctx": lax.rem(place + step + shards, shards)},
            device_id_type=MESH,
        )

    def own_halo(n):
        source, target = ((kv_hbm, xkv), (q_hbm, xq))[n]
        return pltpu.make_async_copy(
            source.at[pl.ds(span_rows - HALO, HALO), :],
            target.at[1, pl.ds(0, HALO), :],
            own_halo_sem.at[n],
        )

    first = place == 0
    last = place == shards - 1
    for n in range(2):

        @pl.when(jnp.logical_not(last))
        def _():
            halo_copy(n, 0, 1).start()

        @pl.when(jnp.logical_not(first))
        def _():
            halo_copy(n, 1, -1).start()

        @pl.when(last)
        def _():
            own_halo(n).start()

    @pl.when(first)
    def _():
        xkv[0, :HALO, :] = jnp.zeros((HALO, xkv.shape[2]), xkv.dtype)
        xq[0, :HALO, :] = jnp.zeros((HALO, xq.shape[2]), xq.dtype)

    for q in range(shards - 1):

        @pl.when(q < place)
        def _():
            gath[2 * shards - 1 - q] = jnp.zeros(gath.shape[1:], gath.dtype)

    def wait_halo(n):
        @pl.when(jnp.logical_not(first))
        def _():
            halo_copy(n, 0, 1).wait_recv()

        @pl.when(jnp.logical_not(last))
        def _():
            halo_copy(n, 1, -1).wait_recv()

        @pl.when(last)
        def _():
            own_halo(n).wait()

    def conv(source, s, i, taps, g):
        columns = pl.ds(g * channels, channels)
        rows = pl.ds(pl.multiple_of(i * block, block), block + HALO)
        x = source[s, rows, columns].astype(jnp.float32)
        w = taps[:, columns]
        total = w[0:1] * x[HALO:]
        for shift in range(1, TAPS):
            total = total + w[shift : shift + 1] * pltpu.roll(x, shift, 0)[HALO:]
        return total.astype(jnp.bfloat16)

    spans = (place, 2 * shards - 1 - place)

    def pair_block(s, i):
        for g in range(2):
            kvc[s * per_span + i, :, g * channels : (g + 1) * channels] = conv(
                xkv, s, i, pt, g
            )
        packed = jnp.dot(
            table[...], kvc[s * per_span + i], preferred_element_type=jnp.float32
        )
        gath[spans[s], pl.ds(pl.multiple_of(i * KEEP, KEEP), KEEP), :] = packed.astype(
            jnp.bfloat16
        )

    def query_block(s, i):
        for h in range(heads):
            qc[s * per_span + i, h] = conv(xq, s, i, qt, h)

    def loop(low, high, body):
        def step(i, carry):
            body(i)
            return carry

        lax.fori_loop(low, high, step, 0)

    small[0].wait()
    small[1].wait()
    for s in range(2):
        loads["kv", s].wait()
        loop(1, per_span, functools.partial(pair_block, s))
    wait_halo(0)
    for s in range(2):
        pair_block(s, 0)

    def span_copy(s, target):
        return pltpu.make_async_remote_copy(
            src_ref=gath.at[spans[s]],
            dst_ref=gath.at[spans[s]],
            send_sem=(lower_send, upper_send)[s].at[target],
            recv_sem=gath_recv.at[spans[s]],
            device_id={"ctx": target},
            device_id_type=MESH,
        )

    for d in range(1, shards):
        span_copy(0, lax.rem(place + d, shards)).start()
    for q in range(shards - 1):

        @pl.when(q < place)
        def _():
            span_copy(1, q).start()

    small[2].wait()
    small[3].wait()
    for s in range(2):
        loads["q", s].wait()
        loop(1, per_span, functools.partial(query_block, s))
    wait_halo(1)
    for s in range(2):
        query_block(s, 0)

    def arrived(span):
        return pltpu.make_async_remote_copy(
            src_ref=gath.at[span],
            dst_ref=gath.at[span],
            send_sem=lower_send.at[0],
            recv_sem=gath_recv.at[span],
            device_id={"ctx": lax.rem(place + 1, shards)},
            device_id_type=MESH,
        )

    scale = math.log2(math.e) / math.sqrt(channels)
    row_id = lax.broadcasted_iota(jnp.int32, (block, block), 0)
    column_id = lax.broadcasted_iota(jnp.int32, (block, block), 1)

    def out_copy(s, i):
        rows = pl.ds(pl.multiple_of((s * per_span + i) * block, block), block)
        return pltpu.make_async_copy(
            out.at[rows, :], out_hbm.at[rows, :], out_sem.at[s * per_span + i]
        )

    def attend(s, i):
        index = s * per_span + i
        far_rows = (s + 1) * shards * half
        query = qc[index].reshape(heads * block, channels)
        near = kvc[index]
        far = gath[: (s + 1) * shards].reshape(far_rows, 2 * channels)
        seen = (spans[s] * per_span + i) * KEEP
        near_bias = jnp.where(row_id >= column_id, 0.0, NEGATIVE)
        far_bias = jnp.where(
            lax.broadcasted_iota(jnp.int32, (1, far_rows), 1) < seen, 0.0, NEGATIVE
        )
        near_scores = nt_dot(query, near[:, :channels])
        near_scores = (
            near_scores.reshape(heads, block, block) + near_bias[None]
        ).reshape(heads * block, block)
        far_scores = nt_dot(query, far[:, :channels]) + far_bias
        scores = jnp.concatenate([near_scores, far_scores], 1)
        top = jnp.max(scores, -1, keepdims=True)
        weights = jnp.exp2((scores - top) * scale).astype(jnp.bfloat16)
        values = jnp.concatenate([near[:, channels:], far[:, channels:]], 0)
        values = jnp.concatenate([values, jnp.ones_like(values)], 1)
        both = jnp.dot(weights, values, preferred_element_type=jnp.float32)
        summed, total = both[:, :channels], both[:, channels:]
        mean = jnp.mean(summed * summed, -1, keepdims=True)
        normed = summed * lax.rsqrt(mean + EPSILON * (total * total))
        rows = pl.ds(pl.multiple_of(index * block, block), block)
        for h in range(heads):
            columns = pl.ds(h * channels, channels)
            out[rows, columns] = (
                normed[h * block : (h + 1) * block] * gain[:, columns]
            ).astype(jnp.bfloat16)
        out_copy(s, i).start()

    for q in range(shards):

        @pl.when(q != place)
        def _():
            arrived(q).wait_recv()

    loop(0, per_span, functools.partial(attend, 0))
    for q in range(1, shards):

        @pl.when(q > place)
        def _():
            arrived(2 * shards - 1 - q).wait_recv()

    loop(0, per_span, functools.partial(attend, 1))

    for s in range(2):
        loop(0, per_span, lambda i: out_copy(s, i).wait())
    for n in range(2):

        @pl.when(jnp.logical_not(last))
        def _():
            halo_copy(n, 0, 1).wait_send()

        @pl.when(jnp.logical_not(first))
        def _():
            halo_copy(n, 1, -1).wait_send()

    for d in range(1, shards):
        span_copy(0, lax.rem(place + d, shards)).wait_send()
    for q in range(shards - 1):

        @pl.when(q < place)
        def _():
            span_copy(1, q).wait_send()


def attention(queries, pairs, query_taps, pair_taps, out_gain, shards):
    rows, columns = queries.shape
    span_rows = rows // 2
    per_span = span_rows // TRANSFORM_BLOCK
    heads = columns // HEAD_CHANNELS
    half = per_span * KEEP
    blocks = 2 * per_span
    bf16, f32 = jnp.bfloat16, jnp.float32
    width = 2 * HEAD_CHANNELS
    anywhere = pl.BlockSpec(memory_space=pl.ANY)
    dma = pltpu.SemaphoreType.DMA
    return pl.pallas_call(
        functools.partial(kernel, shards, per_span, heads),
        out_shape=jax.ShapeDtypeStruct((rows, columns), bf16),
        in_specs=[anywhere] * 6,
        out_specs=anywhere,
        scratch_shapes=[
            pltpu.VMEM((2, HALO + span_rows, columns), bf16),
            pltpu.VMEM((2, HALO + span_rows, width), bf16),
            pltpu.VMEM((TAPS, columns), f32),
            pltpu.VMEM((TAPS, width), f32),
            pltpu.VMEM((1, columns), f32),
            pltpu.VMEM((KEEP, TRANSFORM_BLOCK), bf16),
            pltpu.VMEM((blocks, heads, TRANSFORM_BLOCK, HEAD_CHANNELS), bf16),
            pltpu.VMEM((blocks, TRANSFORM_BLOCK, width), bf16),
            pltpu.VMEM((2 * shards, half, width), bf16),
            pltpu.VMEM((rows, columns), bf16),
            dma((4,)),
            dma((4,)),
            dma((2,)),
            dma((2, 2)),
            dma((2, 2)),
            dma((shards,)),
            dma((shards,)),
            dma((2 * shards,)),
            dma((blocks,)),
        ],
        compiler_params=pltpu.CompilerParams(
            collective_id=0, has_side_effects=True, vmem_limit_bytes=48 * 1024 * 1024
        ),
        name="conv_attention",
    )(
        queries,
        pairs,
        query_taps,
        pair_taps,
        out_gain.reshape(1, columns),
        jnp.asarray(dct_table()),
    )


def from_partner(block, axis, apart):
    count = lax.axis_size(axis)
    route = []
    for low in range(count):
        high = low | 1 << apart
        if high != low and high < count:
            route += [(low, high), (high, low)]
    return lax.ppermute(block, axis, route)


def per_device(queries, keys_values, query_taps, pair_taps, out_gain):
    member = lax.axis_index("mp")
    width = keys_values.shape[1]
    rounds = (2 * HEAD_CHANNELS // width).bit_length() - 1

    def join(mine, bit):
        other = from_partner(mine, "mp", bit)
        lower = member // 2**bit % 2 == 0
        return jnp.where(
            lower, jnp.concatenate([mine, other], 1), jnp.concatenate([other, mine], 1)
        )

    for bit in range(rounds):
        keys_values = join(keys_values, bit)
        pair_taps = join(pair_taps, bit)
    return attention(
        queries, keys_values, query_taps, pair_taps, out_gain, lax.axis_size("ctx")
    )


def solution(mesh):
    in_specs = (P("ctx", "mp"), P("ctx", "mp"), P(None, "mp"), P(None, "mp"), P("mp"))
    out_specs = P("ctx", "mp")
    return jax.shard_map(
        per_device, mesh=mesh, in_specs=in_specs, out_specs=out_specs, check_vma=False
    )
```

```python
import functools
import math

import jax
import jax.numpy as jnp
import numpy as np
from jax import lax
from jax.experimental import pallas as pl
from jax.experimental.pallas import tpu as pltpu
from jax.sharding import PartitionSpec as P

HEAD_CHANNELS = 128
TAPS = 4
TRANSFORM_BLOCK = 128
KEEP = 16
HALO = 16
FAR_PARTS = 4

NEGATIVE = -1e30
EPSILON = 1e-06
MESH = pl.DeviceIdType.MESH


def dct_table():
    frequency = np.arange(KEEP, dtype=np.float32)[:, None]
    offset = np.arange(TRANSFORM_BLOCK, dtype=np.float32)[None, :]
    angle = np.float32(math.pi) * (offset + np.float32(0.5)) * frequency
    table = np.cos(angle / np.float32(TRANSFORM_BLOCK)) * np.float32(
        math.sqrt(2.0 / TRANSFORM_BLOCK)
    )
    table = np.where(frequency == 0.0, table * np.float32(math.sqrt(0.5)), table)
    return table.astype(jnp.bfloat16)


def nt_dot(left, right):
    return lax.dot_general(
        left, right, (((1,), (1,)), ((), ())), preferred_element_type=jnp.float32
    )


def kernel(
    shards,
    per_span,
    heads,
    q_hbm,
    kv_hbm,
    qt_hbm,
    pt_hbm,
    gahbm,
    table_hbm,
    out_hbm,
    xq,
    xkv,
    qt,
    pt,
    gain,
    table,
    qc,
    kvc,
    gath,
    out,
    in_sem,
    small_sem,
    own_halo_sem,
    halo_send,
    halo_recv,
    lower_send,
    upper_send,
    gath_recv,
    lower_first,
    upper_first,
    first_recv,
    out_sem,
):
    place = lax.axis_index("ctx")
    block = TRANSFORM_BLOCK
    span_rows = per_span * block
    half = per_span * KEEP
    channels = HEAD_CHANNELS

    loads = {}
    for s in range(2):
        loads["kv", s] = pltpu.make_async_copy(
            kv_hbm.at[pl.ds(s * span_rows, span_rows), :],
            xkv.at[s, pl.ds(HALO, span_rows), :],
            in_sem.at[s],
        )
        loads["q", s] = pltpu.make_async_copy(
            q_hbm.at[pl.ds(s * span_rows, span_rows), :],
            xq.at[s, pl.ds(HALO, span_rows), :],
            in_sem.at[2 + s],
        )
    small = [
        pltpu.make_async_copy(source, target, small_sem.at[n])
        for n, (source, target) in enumerate(
            [(pt_hbm, pt), (table_hbm, table), (qt_hbm, qt), (gahbm, gain)]
        )
    ]
    loads["kv", 0].start()
    loads["kv", 1].start()
    for copy in small:
        copy.start()
    loads["q", 0].start()
    loads["q", 1].start()

    barrier = pltpu.get_barrier_semaphore()
    for d in range(1, shards):
        pl.semaphore_signal(
            barrier,
            inc=1,
            device_id={"ctx": lax.rem(place + d, shards)},
            device_id_type=MESH,
        )
    pl.semaphore_wait(barrier, shards - 1)

    def halo_copy(n, s, step):
        source, target = ((kv_hbm, xkv), (q_hbm, xq))[n]
        return pltpu.make_async_remote_copy(
            src_ref=source.at[pl.ds((s + 1) * span_rows - HALO, HALO), :],
            dst_ref=target.at[s, pl.ds(0, HALO), :],
            send_sem=halo_send.at[n, s],
            recv_sem=halo_recv.at[n, s],
            device_id={"ctx": lax.rem(place + step + shards, shards)},
            device_id_type=MESH,
        )

    def own_halo(n):
        source, target = ((kv_hbm, xkv), (q_hbm, xq))[n]
        return pltpu.make_async_copy(
            source.at[pl.ds(span_rows - HALO, HALO), :],
            target.at[1, pl.ds(0, HALO), :],
            own_halo_sem.at[n],
        )

    first = place == 0
    last = place == shards - 1
    for n in range(2):

        @pl.when(jnp.logical_not(last))
        def _():
            halo_copy(n, 0, 1).start()

        @pl.when(jnp.logical_not(first))
        def _():
            halo_copy(n, 1, -1).start()

        @pl.when(last)
        def _():
            own_halo(n).start()

    @pl.when(first)
    def _():
        xkv[0, :HALO, :] = jnp.zeros((HALO, xkv.shape[2]), xkv.dtype)
        xq[0, :HALO, :] = jnp.zeros((HALO, xq.shape[2]), xq.dtype)

    for q in range(shards - 1):

        @pl.when(q < place)
        def _():
            gath[2 * shards - 1 - q] = jnp.zeros(gath.shape[1:], gath.dtype)

    def wait_halo(n):
        @pl.when(jnp.logical_not(first))
        def _():
            halo_copy(n, 0, 1).wait_recv()

        @pl.when(jnp.logical_not(last))
        def _():
            halo_copy(n, 1, -1).wait_recv()

        @pl.when(last)
        def _():
            own_halo(n).wait()

    def conv(source, s, i, taps, g):
        columns = pl.ds(g * channels, channels)
        rows = pl.ds(pl.multiple_of(i * block, block), block + HALO)
        x = source[s, rows, columns].astype(jnp.float32)
        w = taps[:, columns]
        back = pltpu.roll(x, 1, 0)
        newer = w[0:1] * x[HALO:] + w[1:2] * back[HALO:]
        older = w[2:3] * x[HALO // 2 :] + w[3:4] * back[HALO // 2 :]
        older = pltpu.roll(older, 2, 0)[HALO // 2 :]
        return (newer + older).astype(jnp.bfloat16)

    spans = (place, 2 * shards - 1 - place)

    def pair_block(s, i):
        for g in range(2):
            kvc[s * per_span + i, :, g * channels : (g + 1) * channels] = conv(
                xkv, s, i, pt, g
            )
        packed = jnp.dot(
            table[...], kvc[s * per_span + i], preferred_element_type=jnp.float32
        )
        gath[spans[s], pl.ds(pl.multiple_of(i * KEEP, KEEP), KEEP), :] = packed.astype(
            jnp.bfloat16
        )

    def query_block(s, i):
        for h in range(heads):
            qc[s * per_span + i, h] = conv(xq, s, i, qt, h)

    def loop(low, high, body):
        def step(i, carry):
            body(i)
            return carry

        lax.fori_loop(low, high, step, 0)

    small[0].wait()
    small[1].wait()
    for s in range(2):
        loads["kv", s].wait()
        loop(1, per_span, functools.partial(pair_block, s))

    def span_copy(s, span, target, part):
        rows = (pl.ds(0, KEEP), pl.ds(KEEP, half - KEEP))[part]
        send = ((lower_first, lower_send), (upper_first, upper_send))[s][part]
        return pltpu.make_async_remote_copy(
            src_ref=gath.at[span, rows, :],
            dst_ref=gath.at[span, rows, :],
            send_sem=send.at[target],
            recv_sem=(first_recv, gath_recv)[part].at[span],
            device_id={"ctx": target},
            device_id_type=MESH,
        )

    def for_each_target(part, act):
        for q in range(shards - 1):

            @pl.when(q < place)
            def _():
                act(span_copy(1, spans[1], q, part))

        for d in range(1, shards):
            act(span_copy(0, spans[0], lax.rem(place + d, shards), part))

    def arrive(s, q):
        span = (q, 2 * shards - 1 - q)[s]
        for part in range(2):
            span_copy(s, span, lax.rem(place + 1, shards), part).wait_recv()

    for_each_target(1, lambda copy: copy.start())
    wait_halo(0)
    for s in range(2):
        pair_block(s, 0)
    for_each_target(0, lambda copy: copy.start())

    small[2].wait()
    small[3].wait()
    for s in range(2):
        loads["q", s].wait()
        loop(1, per_span, functools.partial(query_block, s))
    wait_halo(1)
    for s in range(2):
        query_block(s, 0)

    scale = math.log2(math.e) / math.sqrt(channels)
    row_id = lax.broadcasted_iota(jnp.int32, (block, block), 0)
    column_id = lax.broadcasted_iota(jnp.int32, (block, block), 1)

    part_rows = 2 * shards * half // FAR_PARTS

    def attend(index, parts):
        far_rows = parts * part_rows
        query = qc[index].reshape(heads * block, channels)
        near = kvc[index]
        far = gath[: far_rows // half].reshape(far_rows, 2 * channels)
        near_bias = jnp.where(row_id >= column_id, 0.0, NEGATIVE)
        far_ids = lax.broadcasted_iota(jnp.int32, (1, part_rows), 1)
        far_bias = jnp.where(
            far_ids + (far_rows - part_rows) < block_id(index) * KEEP, 0.0, NEGATIVE
        )
        near_scores = nt_dot(query, near[:, :channels])
        near_scores = (
            near_scores.reshape(heads, block, block) + near_bias[None]
        ).reshape(heads * block, block)
        far_scores = nt_dot(query, far[:, :channels])
        pieces = [near_scores, far_scores[:, far_rows - part_rows :] + far_bias]
        if parts > 1:
            pieces.insert(1, far_scores[:, : far_rows - part_rows])
        scores = jnp.concatenate(pieces, 1)
        top = jnp.max(scores, -1, keepdims=True)
        weights = jnp.exp2((scores - top) * scale).astype(jnp.bfloat16)
        values = jnp.concatenate([near[:, channels:], far[:, channels:]], 0)
        values = jnp.concatenate([values, jnp.ones_like(values)], 1)
        both = jnp.dot(weights, values, preferred_element_type=jnp.float32)
        summed, total = both[:, :channels], both[:, channels:]
        mean = jnp.mean(summed * summed, -1, keepdims=True)
        normed = summed * lax.rsqrt(mean + EPSILON * (total * total))
        rows = pl.ds(pl.multiple_of(index * block, block), block)
        for h in range(heads):
            columns = pl.ds(h * channels, channels)
            out[rows, columns] = (
                normed[h * block : (h + 1) * block] * gain[:, columns]
            ).astype(jnp.bfloat16)

        out_copy(index).start()

    def out_copy(index):
        rows = pl.ds(pl.multiple_of(index * block, block), block)
        return pltpu.make_async_copy(
            out.at[rows, :], out_hbm.at[rows, :], out_sem.at[index]
        )

    def block_id(index):
        upper = index // per_span
        span = place + upper * (2 * shards - 1 - 2 * place)
        return span * per_span + lax.rem(index, per_span)

    for q in range(shards):

        @pl.when(q != place)
        def _():
            arrive(0, q)

    def step(index):
        @pl.when(index == per_span)
        def _():
            for q in range(1, shards):

                @pl.when(q > place)
                def _():
                    arrive(1, q)

        needed = (block_id(index) * KEEP + part_rows - 1) // part_rows
        for parts in range(1, FAR_PARTS + 1):
            fits = needed <= 1 if parts == 1 else needed == parts

            @pl.when(fits)
            def _():
                attend(index, parts)

    loop(0, 2 * per_span, step)
    loop(0, 2 * per_span, lambda index: out_copy(index).wait())

    for n in range(2):

        @pl.when(jnp.logical_not(last))
        def _():
            halo_copy(n, 0, 1).wait_send()

        @pl.when(jnp.logical_not(first))
        def _():
            halo_copy(n, 1, -1).wait_send()

    for part in range(2):
        for_each_target(part, lambda copy: copy.wait_send())


def attention(queries, pairs, query_taps, pair_taps, out_gain, shards):
    rows, columns = queries.shape
    span_rows = rows // 2
    per_span = span_rows // TRANSFORM_BLOCK
    heads = columns // HEAD_CHANNELS
    half = per_span * KEEP
    blocks = 2 * per_span
    bf16, f32 = jnp.bfloat16, jnp.float32
    width = 2 * HEAD_CHANNELS
    hbm = pl.BlockSpec(memory_space=pltpu.HBM)
    dma = pltpu.SemaphoreType.DMA
    return pl.pallas_call(
        functools.partial(kernel, shards, per_span, heads),
        out_shape=jax.ShapeDtypeStruct((rows, columns), bf16),
        in_specs=[hbm] * 6,
        out_specs=hbm,
        scratch_shapes=[
            pltpu.VMEM((2, HALO + span_rows, columns), bf16),
            pltpu.VMEM((2, HALO + span_rows, width), bf16),
            pltpu.VMEM((TAPS, columns), f32),
            pltpu.VMEM((TAPS, width), f32),
            pltpu.VMEM((1, columns), f32),
            pltpu.VMEM((KEEP, TRANSFORM_BLOCK), bf16),
            pltpu.VMEM((blocks, heads, TRANSFORM_BLOCK, HEAD_CHANNELS), bf16),
            pltpu.VMEM((blocks, TRANSFORM_BLOCK, width), bf16),
            pltpu.VMEM((2 * shards, half, width), bf16),
            pltpu.VMEM((rows, columns), bf16),
            dma((4,)),
            dma((4,)),
            dma((2,)),
            dma((2, 2)),
            dma((2, 2)),
            dma((shards,)),
            dma((shards,)),
            dma((2 * shards,)),
            dma((shards,)),
            dma((shards,)),
            dma((2 * shards,)),
            dma((blocks,)),
        ],
        compiler_params=pltpu.CompilerParams(
            collective_id=0, has_side_effects=True, vmem_limit_bytes=62 * 1024 * 1024
        ),
        name="conv_attention",
    )(
        queries,
        pairs,
        query_taps,
        pair_taps,
        out_gain.reshape(1, columns),
        jnp.asarray(dct_table()),
    )


def from_partner(block, axis, apart):
    count = lax.axis_size(axis)
    route = []
    for low in range(count):
        high = low | 1 << apart
        if high != low and high < count:
            route += [(low, high), (high, low)]
    return lax.ppermute(block, axis, route)


def per_device(queries, keys_values, query_taps, pair_taps, out_gain):
    member = lax.axis_index("mp")
    width = keys_values.shape[1]
    rounds = (2 * HEAD_CHANNELS // width).bit_length() - 1

    def join(mine, bit):
        other = from_partner(mine, "mp", bit)
        lower = member // 2**bit % 2 == 0
        return jnp.where(
            lower, jnp.concatenate([mine, other], 1), jnp.concatenate([other, mine], 1)
        )

    for bit in range(rounds):
        keys_values = join(keys_values, bit)
        pair_taps = join(pair_taps, bit)
    return attention(
        queries, keys_values, query_taps, pair_taps, out_gain, lax.axis_size("ctx")
    )


def solution(mesh):
    in_specs = (P("ctx", "mp"), P("ctx", "mp"), P(None, "mp"), P(None, "mp"), P("mp"))
    out_specs = P("ctx", "mp")
    return jax.shard_map(
        per_device, mesh=mesh, in_specs=in_specs, out_specs=out_specs, check_vma=False
    )
```

```python
import functools
import math

import jax
import jax.numpy as jnp
import numpy as np
from jax import lax
from jax.experimental import pallas as pl
from jax.experimental.pallas import tpu as pltpu
from jax.sharding import PartitionSpec as P

HEAD_CHANNELS = 128
TAPS = 4
TRANSFORM_BLOCK = 128
KEEP = 16
HALO = 16
FAR_PARTS = 4

NEGATIVE = -1e30
EPSILON = 1e-06
MESH = pl.DeviceIdType.MESH


def dct_table():
    frequency = np.arange(KEEP, dtype=np.float32)[:, None]
    offset = np.arange(TRANSFORM_BLOCK, dtype=np.float32)[None, :]
    angle = np.float32(math.pi) * (offset + np.float32(0.5)) * frequency
    table = np.cos(angle / np.float32(TRANSFORM_BLOCK)) * np.float32(
        math.sqrt(2.0 / TRANSFORM_BLOCK)
    )
    table = np.where(frequency == 0.0, table * np.float32(math.sqrt(0.5)), table)
    return table.astype(jnp.bfloat16)


def nt_dot(left, right):
    return lax.dot_general(
        left, right, (((1,), (1,)), ((), ())), preferred_element_type=jnp.float32
    )


def kernel(
    shards,
    per_span,
    heads,
    q_hbm,
    kv_hbm,
    qt_hbm,
    pt_hbm,
    gahbm,
    table_hbm,
    out_hbm,
    xq,
    xkv,
    qt,
    pt,
    gain,
    table,
    qc,
    kvc,
    gath,
    out,
    in_sem,
    small_sem,
    own_halo_sem,
    halo_send,
    halo_recv,
    span_send,
    span_recv,
    out_sem,
):
    place = lax.axis_index("ctx")
    block = TRANSFORM_BLOCK
    span_rows = per_span * block
    half = per_span * KEEP
    channels = HEAD_CHANNELS

    loads = {}
    for s in range(2):
        loads["kv", s] = pltpu.make_async_copy(
            kv_hbm.at[pl.ds(s * span_rows, span_rows), :],
            xkv.at[s, pl.ds(HALO, span_rows), :],
            in_sem.at[s],
        )
        loads["q", s] = pltpu.make_async_copy(
            q_hbm.at[pl.ds(s * span_rows, span_rows), :],
            xq.at[s, pl.ds(HALO, span_rows), :],
            in_sem.at[2 + s],
        )
    small = [
        pltpu.make_async_copy(source, target, small_sem.at[n])
        for n, (source, target) in enumerate(
            [(pt_hbm, pt), (table_hbm, table), (qt_hbm, qt), (gahbm, gain)]
        )
    ]
    loads["kv", 0].start()
    loads["kv", 1].start()
    for copy in small:
        copy.start()
    loads["q", 0].start()
    loads["q", 1].start()

    barrier = pltpu.get_barrier_semaphore()
    for d in range(1, shards):
        pl.semaphore_signal(
            barrier,
            inc=1,
            device_id={"ctx": lax.rem(place + d, shards)},
            device_id_type=MESH,
        )
    pl.semaphore_wait(barrier, shards - 1)

    def halo_copy(n, s, step):
        source, target = ((kv_hbm, xkv), (q_hbm, xq))[n]
        return pltpu.make_async_remote_copy(
            src_ref=source.at[pl.ds((s + 1) * span_rows - HALO, HALO), :],
            dst_ref=target.at[s, pl.ds(0, HALO), :],
            send_sem=halo_send.at[n, s],
            recv_sem=halo_recv.at[n, s],
            device_id={"ctx": lax.rem(place + step + shards, shards)},
            device_id_type=MESH,
        )

    def own_halo(n):
        source, target = ((kv_hbm, xkv), (q_hbm, xq))[n]
        return pltpu.make_async_copy(
            source.at[pl.ds(span_rows - HALO, HALO), :],
            target.at[1, pl.ds(0, HALO), :],
            own_halo_sem.at[n],
        )

    first = place == 0
    last = place == shards - 1
    for n in range(2):

        @pl.when(jnp.logical_not(last))
        def _():
            halo_copy(n, 0, 1).start()

        @pl.when(jnp.logical_not(first))
        def _():
            halo_copy(n, 1, -1).start()

        @pl.when(last)
        def _():
            own_halo(n).start()

    @pl.when(first)
    def _():
        xkv[0, :HALO, :] = jnp.zeros((HALO, xkv.shape[2]), xkv.dtype)
        xq[0, :HALO, :] = jnp.zeros((HALO, xq.shape[2]), xq.dtype)

    for q in range(shards - 1):

        @pl.when(q < place)
        def _():
            gath[2 * shards - 1 - q] = jnp.zeros(gath.shape[1:], gath.dtype)

    def wait_halo(n):
        @pl.when(jnp.logical_not(first))
        def _():
            halo_copy(n, 0, 1).wait_recv()

        @pl.when(jnp.logical_not(last))
        def _():
            halo_copy(n, 1, -1).wait_recv()

        @pl.when(last)
        def _():
            own_halo(n).wait()

    def conv(source, s, i, taps, g):
        columns = pl.ds(g * channels, channels)
        rows = pl.ds(pl.multiple_of(i * block, block), block + HALO)
        x = source[s, rows, columns].astype(jnp.float32)
        w = taps[:, columns]
        back = pltpu.roll(x, 1, 0)
        newer = w[0:1] * x[HALO:] + w[1:2] * back[HALO:]
        older = w[2:3] * x[HALO // 2 :] + w[3:4] * back[HALO // 2 :]
        older = pltpu.roll(older, 2, 0)[HALO // 2 :]
        return (newer + older).astype(jnp.bfloat16)

    spans = (place, 2 * shards - 1 - place)

    def pair_block(s, i):
        for g in range(2):
            kvc[s * per_span + i, :, g * channels : (g + 1) * channels] = conv(
                xkv, s, i, pt, g
            )
        packed = jnp.dot(
            table[...], kvc[s * per_span + i], preferred_element_type=jnp.float32
        )
        gath[spans[s], pl.ds(pl.multiple_of(i * KEEP, KEEP), KEEP), :] = packed.astype(
            jnp.bfloat16
        )

    def query_block(s, i):
        for h in range(heads):
            qc[s * per_span + i, h] = conv(xq, s, i, qt, h)

    def loop(low, high, body):
        def step(i, carry):
            body(i)
            return carry

        lax.fori_loop(low, high, step, 0)

    small[0].wait()
    small[1].wait()
    for s in range(2):
        loads["kv", s].wait()
        loop(1, per_span, functools.partial(pair_block, s))

    mate = place + 1 - 2 * lax.rem(place, 2)
    chips = shards // 2

    def peer(d):
        return lax.rem(place + 2 * d, shards)

    def span_copy(s, span, target, part, hop):
        rows = (pl.ds(0, KEEP), pl.ds(KEEP, half - KEEP))[part]
        return pltpu.make_async_remote_copy(
            src_ref=gath.at[span, rows, :],
            dst_ref=gath.at[span, rows, :],
            send_sem=span_send.at[part, s, hop],
            recv_sem=span_recv.at[part, span],
            device_id={"ctx": target},
            device_id_type=MESH,
        )

    def when(condition, act):
        @pl.when(condition)
        def _():
            act()

    def own_copies(part, act):
        for d in range(1, chips):
            target = peer(d)
            act(span_copy(0, spans[0], target, part, d))
            when(target < place, lambda: act(span_copy(1, spans[1], target, part, d)))
        act(span_copy(0, spans[0], mate, part, 0))
        when(mate < place, lambda: act(span_copy(1, spans[1], mate, part, 0)))

    def passed_copies(part, d, act):
        source = peer(d)
        hop = chips - 1 + d
        act(span_copy(0, source, mate, part, hop))
        upper = 2 * shards - 1 - source
        when(source > place, lambda: act(span_copy(1, upper, mate, part, hop)))

    def arrive(s, q, part):
        span = (q, 2 * shards - 1 - q)[s]
        span_copy(s, span, mate, part, 0).wait_recv()

    def pass_on(part):
        for d in range(1, chips):
            source = peer(d)
            arrive(0, source, part)
            when(source > place, lambda: arrive(1, source, part))
            passed_copies(part, d, lambda copy: copy.start())

    own_copies(1, lambda copy: copy.start())
    wait_halo(0)
    for s in range(2):
        pair_block(s, 0)
    own_copies(0, lambda copy: copy.start())

    small[2].wait()
    small[3].wait()
    for s in range(2):
        loads["q", s].wait()
        loop(1, per_span, functools.partial(query_block, s))
    wait_halo(1)
    for s in range(2):
        query_block(s, 0)

    scale = math.log2(math.e) / math.sqrt(channels)
    row_id = lax.broadcasted_iota(jnp.int32, (block, block), 0)
    column_id = lax.broadcasted_iota(jnp.int32, (block, block), 1)

    part_rows = 2 * shards * half // FAR_PARTS

    def attend(index, parts):
        far_rows = parts * part_rows
        near = kvc[index]
        far = gath[: far_rows // half].reshape(far_rows, 2 * channels)
        near_bias = jnp.where(row_id >= column_id, 0.0, NEGATIVE)
        far_ids = lax.broadcasted_iota(jnp.int32, (1, part_rows), 1)
        far_bias = jnp.where(
            far_ids + (far_rows - part_rows) < block_id(index) * KEEP, 0.0, NEGATIVE
        )
        values = jnp.concatenate([near[:, channels:], far[:, channels:]], 0)
        values = jnp.concatenate([values, jnp.ones_like(values)], 1)
        rows = pl.ds(pl.multiple_of(index * block, block), block)
        some = min(heads, 2)
        for begin in range(0, heads, some):
            query = qc[index, begin : begin + some].reshape(some * block, channels)
            near_scores = nt_dot(query, near[:, :channels])
            near_scores = (
                near_scores.reshape(some, block, block) + near_bias[None]
            ).reshape(some * block, block)
            far_scores = nt_dot(query, far[:, :channels])
            pieces = [near_scores, far_scores[:, far_rows - part_rows :] + far_bias]
            if parts > 1:
                pieces.insert(1, far_scores[:, : far_rows - part_rows])
            scores = jnp.concatenate(pieces, 1)
            top = jnp.max(scores, -1, keepdims=True)
            weights = jnp.exp2((scores - top) * scale).astype(jnp.bfloat16)
            both = jnp.dot(weights, values, preferred_element_type=jnp.float32)
            summed, total = both[:, :channels], both[:, channels:]
            mean = jnp.mean(summed * summed, -1, keepdims=True)
            normed = summed * lax.rsqrt(mean + EPSILON * (total * total))
            for h in range(some):
                columns = pl.ds((begin + h) * channels, channels)
                out[rows, columns] = (
                    normed[h * block : (h + 1) * block] * gain[:, columns]
                ).astype(jnp.bfloat16)
        out_copy(index).start()

    def out_copy(index):
        rows = pl.ds(pl.multiple_of(index * block, block), block)
        return pltpu.make_async_copy(
            out.at[rows, :], out_hbm.at[rows, :], out_sem.at[index]
        )

    def block_id(index):
        upper = index // per_span
        span = place + upper * (2 * shards - 1 - 2 * place)
        return span * per_span + lax.rem(index, per_span)

    def from_mate(s, q):
        return jnp.logical_and(
            lax.rem(q, 2) == lax.rem(mate, 2), (q >= 0) if s == 0 else (q > place)
        )

    def needed_parts(index):
        return (block_id(index) * KEEP + part_rows - 1) // part_rows

    lower_spans = needed_parts(per_span - 1) * (part_rows // half)

    def await_spans(s, low, high):
        for q in range(shards):
            wanted = jnp.logical_and(q >= low, q < high)

            @pl.when(jnp.logical_and(wanted, from_mate(s, q)))
            def _():
                for part in range(2):
                    arrive(s, q, part)

    pass_on(1)
    pass_on(0)
    await_spans(0, 0, lower_spans)

    def step(index):
        @pl.when(index == per_span)
        def _():
            await_spans(0, lower_spans, shards)
            await_spans(1, 0, shards)

        needed = needed_parts(index)
        for parts in range(1, FAR_PARTS + 1):
            fits = needed <= 1 if parts == 1 else needed == parts

            @pl.when(fits)
            def _():
                attend(index, parts)

    loop(0, 2 * per_span, step)
    loop(0, 2 * per_span, lambda index: out_copy(index).wait())

    for n in range(2):

        @pl.when(jnp.logical_not(last))
        def _():
            halo_copy(n, 0, 1).wait_send()

        @pl.when(jnp.logical_not(first))
        def _():
            halo_copy(n, 1, -1).wait_send()

    for part in range(2):
        own_copies(part, lambda copy: copy.wait_send())
        for d in range(1, chips):
            passed_copies(part, d, lambda copy: copy.wait_send())


def attention(queries, pairs, query_taps, pair_taps, out_gain, shards):
    rows, columns = queries.shape
    span_rows = rows // 2
    per_span = span_rows // TRANSFORM_BLOCK
    heads = columns // HEAD_CHANNELS
    half = per_span * KEEP
    blocks = 2 * per_span
    bf16, f32 = jnp.bfloat16, jnp.float32
    width = 2 * HEAD_CHANNELS
    hbm = pl.BlockSpec(memory_space=pltpu.HBM)
    dma = pltpu.SemaphoreType.DMA
    return pl.pallas_call(
        functools.partial(kernel, shards, per_span, heads),
        out_shape=jax.ShapeDtypeStruct((rows, columns), bf16),
        in_specs=[hbm] * 6,
        out_specs=hbm,
        scratch_shapes=[
            pltpu.VMEM((2, HALO + span_rows, columns), bf16),
            pltpu.VMEM((2, HALO + span_rows, width), bf16),
            pltpu.VMEM((TAPS, columns), f32),
            pltpu.VMEM((TAPS, width), f32),
            pltpu.VMEM((1, columns), f32),
            pltpu.VMEM((KEEP, TRANSFORM_BLOCK), bf16),
            pltpu.VMEM((blocks, heads, TRANSFORM_BLOCK, HEAD_CHANNELS), bf16),
            pltpu.VMEM((blocks, TRANSFORM_BLOCK, width), bf16),
            pltpu.VMEM((2 * shards, half, width), bf16),
            pltpu.VMEM((rows, columns), bf16),
            dma((4,)),
            dma((4,)),
            dma((2,)),
            dma((2, 2)),
            dma((2, 2)),
            dma((2, 2, shards)),
            dma((2, 2 * shards)),
            dma((blocks,)),
        ],
        compiler_params=pltpu.CompilerParams(
            collective_id=0, has_side_effects=True, vmem_limit_bytes=62 * 1024 * 1024
        ),
        name="conv_attention",
    )(
        queries,
        pairs,
        query_taps,
        pair_taps,
        out_gain.reshape(1, columns),
        jnp.asarray(dct_table()),
    )


def from_partner(block, axis, apart):
    count = lax.axis_size(axis)
    route = []
    for low in range(count):
        high = low | 1 << apart
        if high != low and high < count:
            route += [(low, high), (high, low)]
    return lax.ppermute(block, axis, route)


def per_device(queries, keys_values, query_taps, pair_taps, out_gain):
    member = lax.axis_index("mp")
    width = keys_values.shape[1]
    rounds = (2 * HEAD_CHANNELS // width).bit_length() - 1

    def join(mine, bit):
        other = from_partner(mine, "mp", bit)
        lower = member // 2**bit % 2 == 0
        return jnp.where(
            lower, jnp.concatenate([mine, other], 1), jnp.concatenate([other, mine], 1)
        )

    for bit in range(rounds):
        keys_values = join(keys_values, bit)
        pair_taps = join(pair_taps, bit)
    return attention(
        queries, keys_values, query_taps, pair_taps, out_gain, lax.axis_size("ctx")
    )


def solution(mesh):
    in_specs = (P("ctx", "mp"), P("ctx", "mp"), P(None, "mp"), P(None, "mp"), P("mp"))
    out_specs = P("ctx", "mp")
    return jax.shard_map(
        per_device, mesh=mesh, in_specs=in_specs, out_specs=out_specs, check_vma=False
    )
```

```python
import functools
import math

import jax
import jax.numpy as jnp
import numpy as np
from jax import lax
from jax.experimental import pallas as pl
from jax.experimental.pallas import tpu as pltpu
from jax.sharding import PartitionSpec as P

HEAD_CHANNELS = 128
TAPS = 4
TRANSFORM_BLOCK = 128
KEEP = 16
HALO = 16
FAR_PARTS = 4

NEGATIVE = -1e30
EPSILON = 1e-06
MESH = pl.DeviceIdType.MESH


def dct_table():
    frequency = np.arange(KEEP, dtype=np.float32)[:, None]
    offset = np.arange(TRANSFORM_BLOCK, dtype=np.float32)[None, :]
    angle = np.float32(math.pi) * (offset + np.float32(0.5)) * frequency
    table = np.cos(angle / np.float32(TRANSFORM_BLOCK)) * np.float32(
        math.sqrt(2.0 / TRANSFORM_BLOCK)
    )
    table = np.where(frequency == 0.0, table * np.float32(math.sqrt(0.5)), table)
    return table.astype(jnp.bfloat16)


def nt_dot(left, right):
    return lax.dot_general(
        left, right, (((1,), (1,)), ((), ())), preferred_element_type=jnp.float32
    )


def loop(low, high, body):
    def step(i, carry):
        body(i)
        return carry

    lax.fori_loop(low, high, step, 0)


def block_of(place, shards, per_span, index):
    upper = index // per_span
    span = place + upper * (2 * shards - 1 - 2 * place)
    return span * per_span + lax.rem(index, per_span)


def attend_block(qc, kvc, gath, gain, out, index, block_id, part_rows, least, most):
    needed = (block_id * KEEP + part_rows - 1) // part_rows
    for parts in range(least, most + 1):
        fits = needed <= least if parts == least else needed == parts

        @pl.when(fits)
        def _():
            attend(qc, kvc, gath, gain, out, index, block_id, part_rows, parts)


def attend(qc, kvc, gath, gain, out, index, block_id, part_rows, parts):
    block, channels = TRANSFORM_BLOCK, HEAD_CHANNELS
    heads, half = qc.shape[1], gath.shape[1]
    scale = math.log2(math.e) / math.sqrt(channels)
    row_id = lax.broadcasted_iota(jnp.int32, (block, block), 0)
    column_id = lax.broadcasted_iota(jnp.int32, (block, block), 1)
    far_rows = parts * part_rows
    near = kvc[index]
    far = gath[: far_rows // half].reshape(far_rows, 2 * channels)
    near_bias = jnp.where(row_id >= column_id, 0.0, NEGATIVE)
    far_ids = lax.broadcasted_iota(jnp.int32, (1, part_rows), 1)
    far_bias = jnp.where(
        far_ids + (far_rows - part_rows) < block_id * KEEP, 0.0, NEGATIVE
    )
    values = jnp.concatenate([near[:, channels:], far[:, channels:]], 0)
    values = jnp.concatenate([values, jnp.ones_like(values)], 1)
    rows = pl.ds(pl.multiple_of(index * block, block), block)
    some = min(heads, 2)
    for begin in range(0, heads, some):
        query = qc[index, begin : begin + some].reshape(some * block, channels)
        near_scores = nt_dot(query, near[:, :channels])
        near_scores = (
            near_scores.reshape(some, block, block) + near_bias[None]
        ).reshape(some * block, block)
        far_scores = nt_dot(query, far[:, :channels])
        pieces = [near_scores, far_scores[:, far_rows - part_rows :] + far_bias]
        if parts > 1:
            pieces.insert(1, far_scores[:, : far_rows - part_rows])
        scores = jnp.concatenate(pieces, 1)
        top = jnp.max(scores, -1, keepdims=True)
        weights = jnp.exp2((scores - top) * scale).astype(jnp.bfloat16)
        both = jnp.dot(weights, values, preferred_element_type=jnp.float32)
        summed, total = both[:, :channels], both[:, channels:]
        mean = jnp.mean(summed * summed, -1, keepdims=True)
        normed = summed * lax.rsqrt(mean + EPSILON * (total * total))
        for h in range(some):
            columns = pl.ds((begin + h) * channels, channels)
            out[rows, columns] = (
                normed[h * block : (h + 1) * block] * gain[:, columns]
            ).astype(jnp.bfloat16)


def kernel(
    shards,
    per_span,
    heads,
    q_hbm,
    kv_hbm,
    qt_hbm,
    pt_hbm,
    gahbm,
    table_hbm,
    low_hbm,
    qc_hbm,
    kvc_hbm,
    gath_hbm,
    xq,
    xkv,
    qt,
    pt,
    gain,
    table,
    qc,
    kvc,
    gath,
    out,
    in_sem,
    small_sem,
    own_halo_sem,
    halo_send,
    halo_recv,
    span_send,
    span_recv,
    out_sem,
    hand_sem,
):
    place = lax.axis_index("ctx")
    block = TRANSFORM_BLOCK
    span_rows = per_span * block
    half = per_span * KEEP
    channels = HEAD_CHANNELS

    loads = {}
    for s in range(2):
        loads["kv", s] = pltpu.make_async_copy(
            kv_hbm.at[pl.ds(s * span_rows, span_rows), :],
            xkv.at[s, pl.ds(HALO, span_rows), :],
            in_sem.at[s],
        )
        loads["q", s] = pltpu.make_async_copy(
            q_hbm.at[pl.ds(s * span_rows, span_rows), :],
            xq.at[s, pl.ds(HALO, span_rows), :],
            in_sem.at[2 + s],
        )
    small = [
        pltpu.make_async_copy(source, target, small_sem.at[n])
        for n, (source, target) in enumerate(
            [(pt_hbm, pt), (table_hbm, table), (qt_hbm, qt), (gahbm, gain)]
        )
    ]
    loads["kv", 0].start()
    loads["kv", 1].start()
    for copy in small:
        copy.start()
    loads["q", 0].start()
    loads["q", 1].start()

    barrier = pltpu.get_barrier_semaphore()
    for d in range(1, shards):
        pl.semaphore_signal(
            barrier,
            inc=1,
            device_id={"ctx": lax.rem(place + d, shards)},
            device_id_type=MESH,
        )
    pl.semaphore_wait(barrier, shards - 1)

    def halo_copy(n, s, step):
        source, target = ((kv_hbm, xkv), (q_hbm, xq))[n]
        return pltpu.make_async_remote_copy(
            src_ref=source.at[pl.ds((s + 1) * span_rows - HALO, HALO), :],
            dst_ref=target.at[s, pl.ds(0, HALO), :],
            send_sem=halo_send.at[n, s],
            recv_sem=halo_recv.at[n, s],
            device_id={"ctx": lax.rem(place + step + shards, shards)},
            device_id_type=MESH,
        )

    def own_halo(n):
        source, target = ((kv_hbm, xkv), (q_hbm, xq))[n]
        return pltpu.make_async_copy(
            source.at[pl.ds(span_rows - HALO, HALO), :],
            target.at[1, pl.ds(0, HALO), :],
            own_halo_sem.at[n],
        )

    first = place == 0
    last = place == shards - 1
    for n in range(2):

        @pl.when(jnp.logical_not(last))
        def _():
            halo_copy(n, 0, 1).start()

        @pl.when(jnp.logical_not(first))
        def _():
            halo_copy(n, 1, -1).start()

        @pl.when(last)
        def _():
            own_halo(n).start()

    @pl.when(first)
    def _():
        xkv[0, :HALO, :] = jnp.zeros((HALO, xkv.shape[2]), xkv.dtype)
        xq[0, :HALO, :] = jnp.zeros((HALO, xq.shape[2]), xq.dtype)

    for q in range(shards - 1):

        @pl.when(q < place)
        def _():
            gath[2 * shards - 1 - q] = jnp.zeros(gath.shape[1:], gath.dtype)

    def wait_halo(n):
        @pl.when(jnp.logical_not(first))
        def _():
            halo_copy(n, 0, 1).wait_recv()

        @pl.when(jnp.logical_not(last))
        def _():
            halo_copy(n, 1, -1).wait_recv()

        @pl.when(last)
        def _():
            own_halo(n).wait()

    def conv(source, s, i, taps, g):
        columns = pl.ds(g * channels, channels)
        rows = pl.ds(pl.multiple_of(i * block, block), block + HALO)
        x = source[s, rows, columns].astype(jnp.float32)
        w = taps[:, columns]
        back = pltpu.roll(x, 1, 0)
        newer = w[0:1] * x[HALO:] + w[1:2] * back[HALO:]
        older = w[2:3] * x[HALO // 2 :] + w[3:4] * back[HALO // 2 :]
        older = pltpu.roll(older, 2, 0)[HALO // 2 :]
        return (newer + older).astype(jnp.bfloat16)

    spans = (place, 2 * shards - 1 - place)

    def pair_block(s, i):
        for g in range(2):
            kvc[s * per_span + i, :, g * channels : (g + 1) * channels] = conv(
                xkv, s, i, pt, g
            )
        packed = jnp.dot(
            table[...], kvc[s * per_span + i], preferred_element_type=jnp.float32
        )
        gath[spans[s], pl.ds(pl.multiple_of(i * KEEP, KEEP), KEEP), :] = packed.astype(
            jnp.bfloat16
        )

    def query_block(s, i):
        for h in range(heads):
            qc[s * per_span + i, h] = conv(xq, s, i, qt, h)

    small[0].wait()
    small[1].wait()
    for s in range(2):
        loads["kv", s].wait()
        loop(1, per_span, functools.partial(pair_block, s))

    mate = place + 1 - 2 * lax.rem(place, 2)
    chips = shards // 2

    def peer(d):
        return lax.rem(place + 2 * d, shards)

    def span_copy(s, span, target, part, hop):
        rows = (pl.ds(0, KEEP), pl.ds(KEEP, half - KEEP))[part]
        return pltpu.make_async_remote_copy(
            src_ref=gath.at[span, rows, :],
            dst_ref=gath.at[span, rows, :],
            send_sem=span_send.at[part, s, hop],
            recv_sem=span_recv.at[part, span],
            device_id={"ctx": target},
            device_id_type=MESH,
        )

    def when(condition, act):
        @pl.when(condition)
        def _():
            act()

    def own_copies(part, act):
        for d in range(1, chips):
            target = peer(d)
            other = target + 1 - 2 * lax.rem(target, 2)
            act(span_copy(0, spans[0], target, part, d))
            when(
                target > place,
                lambda: act(span_copy(0, spans[0], other, part, shards + d)),
            )
            when(target < place, lambda: act(span_copy(1, spans[1], target, part, d)))
        act(span_copy(0, spans[0], mate, part, 0))
        when(mate < place, lambda: act(span_copy(1, spans[1], mate, part, 0)))

    def passed_copies(part, d, act):
        source = peer(d)
        upper = 2 * shards - 1 - source

        def both():
            act(span_copy(0, source, mate, part, shards + chips + d))
            act(span_copy(1, upper, mate, part, shards + chips + d))

        when(source > place, both)

    def arrive(s, q, part):
        span = (q, 2 * shards - 1 - q)[s]
        span_copy(s, span, mate, part, 0).wait_recv()

    def pass_on(part):
        for d in range(1, chips):
            source = peer(d)

            def both():
                arrive(0, source, part)
                arrive(1, source, part)

            when(source > place, both)
            passed_copies(part, d, lambda copy: copy.start())

    own_copies(1, lambda copy: copy.start())
    wait_halo(0)
    for s in range(2):
        pair_block(s, 0)
    own_copies(0, lambda copy: copy.start())

    small[2].wait()
    small[3].wait()
    for s in range(2):
        loads["q", s].wait()
        loop(1, per_span, functools.partial(query_block, s))
    wait_halo(1)
    for s in range(2):
        query_block(s, 0)

    block_id = functools.partial(block_of, place, shards, per_span)
    part_rows = 2 * shards * half // FAR_PARTS

    def low_copy(i):
        rows = pl.ds(pl.multiple_of(i * block, block), block)
        return pltpu.make_async_copy(out.at[rows, :], low_hbm.at[rows, :], out_sem.at[i])

    def awaited(s, q):
        passed = jnp.logical_and(lax.rem(q, 2) == lax.rem(place, 2), q > place)
        return jnp.logical_and(jnp.logical_not(passed), (q != place) if s == 0 else (q > place))

    def needed_parts(index):
        return (block_id(index) * KEEP + part_rows - 1) // part_rows

    lower_spans = needed_parts(per_span - 1) * (part_rows // half)

    def await_spans(s, low, high):
        for q in range(shards):
            wanted = jnp.logical_and(q >= low, q < high)

            @pl.when(jnp.logical_and(wanted, awaited(s, q)))
            def _():
                for part in range(2):
                    arrive(s, q, part)

    handed = [
        pltpu.make_async_copy(source, target, hand_sem.at[n])
        for n, (source, target) in enumerate(
            [
                (qc.at[pl.ds(per_span, per_span)], qc_hbm),
                (kvc.at[pl.ds(per_span, per_span)], kvc_hbm),
                (gath, gath_hbm),
            ]
        )
    ]
    handed[0].start()
    handed[1].start()

    early = lower_spans > place - lax.rem(place, 2) + 2

    @pl.when(early)
    def _():
        pass_on(1)
        pass_on(0)

    await_spans(0, 0, lower_spans)

    def step(index):
        @pl.when(jnp.logical_and(index == min(1, per_span - 1), jnp.logical_not(early)))
        def _():
            pass_on(1)
            pass_on(0)

        @pl.when(index == per_span - 1)
        def _():
            await_spans(0, lower_spans, shards)
            await_spans(1, 0, shards)
            handed[2].start()

        attend_block(
            qc, kvc, gath, gain, out, index, block_id(index), part_rows, 1, FAR_PARTS // 2
        )
        low_copy(index).start()

    loop(0, per_span, step)
    loop(0, per_span, lambda index: low_copy(index).wait())
    for copy in handed:
        copy.wait()

    for n in range(2):

        @pl.when(jnp.logical_not(last))
        def _():
            halo_copy(n, 0, 1).wait_send()

        @pl.when(jnp.logical_not(first))
        def _():
            halo_copy(n, 1, -1).wait_send()

    for part in range(2):
        own_copies(part, lambda copy: copy.wait_send())
        for d in range(1, chips):
            passed_copies(part, d, lambda copy: copy.wait_send())


def upper_kernel(
    shards,
    per_span,
    heads,
    low_hbm,
    qc_hbm,
    kvc_hbm,
    gath_hbm,
    gain_hbm,
    out_hbm,
    qc,
    kvc,
    gath,
    gain,
    out,
    in_sem,
    q_sem,
    out_sem,
    low_sem,
):
    place = lax.axis_index("ctx")
    block = TRANSFORM_BLOCK
    span_rows = per_span * block
    part_rows = 2 * shards * per_span * KEEP // FAR_PARTS

    loads = [
        pltpu.make_async_copy(source, target, in_sem.at[n])
        for n, (source, target) in enumerate(
            [(gath_hbm, gath), (kvc_hbm, kvc), (gain_hbm, gain)]
        )
    ]

    def query_load(i):
        return pltpu.make_async_copy(qc_hbm.at[i], qc.at[i], q_sem.at[i])

    query_load(0).start()
    for copy in loads:
        copy.start()
    loop(1, per_span, lambda i: query_load(i).start())
    low_copy = pltpu.make_async_copy(
        low_hbm, out_hbm.at[pl.ds(0, span_rows), :], low_sem
    )
    low_copy.start()

    def out_copy(i):
        rows = pl.ds(pl.multiple_of(i * block, block), block)
        target = pl.ds(pl.multiple_of(span_rows + i * block, block), block)
        return pltpu.make_async_copy(
            out.at[rows, :], out_hbm.at[target, :], out_sem.at[i]
        )

    for copy in loads:
        copy.wait()

    def step(i):
        query_load(i).wait()
        block_id = block_of(place, shards, per_span, per_span + i)
        attend_block(
            qc, kvc, gath, gain, out, i, block_id, part_rows, FAR_PARTS // 2, FAR_PARTS
        )
        out_copy(i).start()

    loop(0, per_span, step)
    loop(0, per_span, lambda i: out_copy(i).wait())
    low_copy.wait()


def attention(queries, pairs, query_taps, pair_taps, out_gain, shards):
    rows, columns = queries.shape
    span_rows = rows // 2
    per_span = span_rows // TRANSFORM_BLOCK
    heads = columns // HEAD_CHANNELS
    half = per_span * KEEP
    blocks = 2 * per_span
    bf16, f32 = jnp.bfloat16, jnp.float32
    width = 2 * HEAD_CHANNELS
    hbm = pl.BlockSpec(memory_space=pltpu.HBM)
    dma = pltpu.SemaphoreType.DMA
    gain = out_gain.reshape(1, columns)
    half_q = (per_span, heads, TRANSFORM_BLOCK, HEAD_CHANNELS)
    half_kv = (per_span, TRANSFORM_BLOCK, width)
    all_packed = (2 * shards, half, width)
    handed = pl.pallas_call(
        functools.partial(kernel, shards, per_span, heads),
        out_shape=[
            jax.ShapeDtypeStruct((span_rows, columns), bf16),
            jax.ShapeDtypeStruct(half_q, bf16),
            jax.ShapeDtypeStruct(half_kv, bf16),
            jax.ShapeDtypeStruct(all_packed, bf16),
        ],
        in_specs=[hbm] * 6,
        out_specs=[hbm] * 4,
        scratch_shapes=[
            pltpu.VMEM((2, HALO + span_rows, columns), bf16),
            pltpu.VMEM((2, HALO + span_rows, width), bf16),
            pltpu.VMEM((TAPS, columns), f32),
            pltpu.VMEM((TAPS, width), f32),
            pltpu.VMEM((1, columns), f32),
            pltpu.VMEM((KEEP, TRANSFORM_BLOCK), bf16),
            pltpu.VMEM((blocks, heads, TRANSFORM_BLOCK, HEAD_CHANNELS), bf16),
            pltpu.VMEM((blocks, TRANSFORM_BLOCK, width), bf16),
            pltpu.VMEM(all_packed, bf16),
            pltpu.VMEM((span_rows, columns), bf16),
            dma((4,)),
            dma((4,)),
            dma((2,)),
            dma((2, 2)),
            dma((2, 2)),
            dma((2, 2, 2 * shards)),
            dma((2, 2 * shards)),
            dma((per_span,)),
            dma((3,)),
        ],
        compiler_params=pltpu.CompilerParams(
            collective_id=0, has_side_effects=True, vmem_limit_bytes=62 * 1024 * 1024
        ),
        name="exchange_and_lower",
    )(
        queries,
        pairs,
        query_taps,
        pair_taps,
        gain,
        jnp.asarray(dct_table()),
    )
    return pl.pallas_call(
        functools.partial(upper_kernel, shards, per_span, heads),
        out_shape=jax.ShapeDtypeStruct((rows, columns), bf16),
        in_specs=[hbm] * 5,
        out_specs=hbm,
        scratch_shapes=[
            pltpu.VMEM(half_q, bf16),
            pltpu.VMEM(half_kv, bf16),
            pltpu.VMEM(all_packed, bf16),
            pltpu.VMEM((1, columns), f32),
            pltpu.VMEM((span_rows, columns), bf16),
            dma((3,)),
            dma((per_span,)),
            dma((per_span,)),
            dma,
        ],
        compiler_params=pltpu.CompilerParams(vmem_limit_bytes=62 * 1024 * 1024),
        name="upper",
    )(*handed, gain)


def from_partner(block, axis, apart):
    count = lax.axis_size(axis)
    route = []
    for low in range(count):
        high = low | 1 << apart
        if high != low and high < count:
            route += [(low, high), (high, low)]
    return lax.ppermute(block, axis, route)


def per_device(queries, keys_values, query_taps, pair_taps, out_gain):
    member = lax.axis_index("mp")
    width = keys_values.shape[1]
    rounds = (2 * HEAD_CHANNELS // width).bit_length() - 1

    def join(mine, bit):
        other = from_partner(mine, "mp", bit)
        lower = member // 2**bit % 2 == 0
        return jnp.where(
            lower, jnp.concatenate([mine, other], 1), jnp.concatenate([other, mine], 1)
        )

    for bit in range(rounds):
        keys_values = join(keys_values, bit)
        pair_taps = join(pair_taps, bit)
    return attention(
        queries, keys_values, query_taps, pair_taps, out_gain, lax.axis_size("ctx")
    )


def solution(mesh):
    in_specs = (P("ctx", "mp"), P("ctx", "mp"), P(None, "mp"), P(None, "mp"), P("mp"))
    out_specs = P("ctx", "mp")
    return jax.shard_map(
        per_device, mesh=mesh, in_specs=in_specs, out_specs=out_specs, check_vma=False
    )
```

```python
import functools
import math

import jax
import jax.numpy as jnp
import numpy as np
from jax import lax
from jax.experimental import pallas as pl
from jax.experimental.pallas import tpu as pltpu
from jax.sharding import PartitionSpec as P

HEAD_CHANNELS = 128
TAPS = 4
TRANSFORM_BLOCK = 128
KEEP = 16
HALO = 16
FAR_PARTS = 4

NEGATIVE = -1e30
EPSILON = 1e-06
MESH = pl.DeviceIdType.MESH


def dct_table():
    frequency = np.arange(KEEP, dtype=np.float32)[:, None]
    offset = np.arange(TRANSFORM_BLOCK, dtype=np.float32)[None, :]
    angle = np.float32(math.pi) * (offset + np.float32(0.5)) * frequency
    table = np.cos(angle / np.float32(TRANSFORM_BLOCK)) * np.float32(
        math.sqrt(2.0 / TRANSFORM_BLOCK)
    )
    table = np.where(frequency == 0.0, table * np.float32(math.sqrt(0.5)), table)
    return table.astype(jnp.bfloat16)


def nt_dot(left, right):
    return lax.dot_general(
        left, right, (((1,), (1,)), ((), ())), preferred_element_type=jnp.float32
    )


def loop(low, high, body):
    def step(i, carry):
        body(i)
        return carry

    lax.fori_loop(low, high, step, 0)


def block_of(place, shards, per_span, index):
    upper = index // per_span
    span = place + upper * (2 * shards - 1 - 2 * place)
    return span * per_span + lax.rem(index, per_span)


def attend_block(qc, kvc, gath, gain, out, index, block_id, part_rows, least, most):
    needed = (block_id * KEEP + part_rows - 1) // part_rows
    for parts in range(least, most + 1):
        fits = needed <= least if parts == least else needed == parts

        @pl.when(fits)
        def _():
            attend(qc, kvc, gath, gain, out, index, block_id, part_rows, parts)


def attend(qc, kvc, gath, gain, out, index, block_id, part_rows, parts):
    block, channels = TRANSFORM_BLOCK, HEAD_CHANNELS
    heads, half = qc.shape[1], gath.shape[1]
    scale = math.log2(math.e) / math.sqrt(channels)
    row_id = lax.broadcasted_iota(jnp.int32, (block, block), 0)
    column_id = lax.broadcasted_iota(jnp.int32, (block, block), 1)
    far_rows = parts * part_rows
    near = kvc[index]
    far = gath[: far_rows // half].reshape(far_rows, 2 * channels)
    near_bias = jnp.where(row_id >= column_id, 0.0, NEGATIVE)
    far_ids = lax.broadcasted_iota(jnp.int32, (1, part_rows), 1)
    far_bias = jnp.where(
        far_ids + (far_rows - part_rows) < block_id * KEEP, 0.0, NEGATIVE
    )
    values = jnp.concatenate([near[:, channels:], far[:, channels:]], 0)
    values = jnp.concatenate([values, jnp.ones_like(values)], 1)
    rows = pl.ds(pl.multiple_of(index * block, block), block)
    some = min(heads, 2)
    for begin in range(0, heads, some):
        query = qc[index, begin : begin + some].reshape(some * block, channels)
        near_scores = nt_dot(query, near[:, :channels])
        near_scores = (
            near_scores.reshape(some, block, block) + near_bias[None]
        ).reshape(some * block, block)
        far_scores = nt_dot(query, far[:, :channels])
        pieces = [near_scores, far_scores[:, far_rows - part_rows :] + far_bias]
        if parts > 1:
            pieces.insert(1, far_scores[:, : far_rows - part_rows])
        scores = jnp.concatenate(pieces, 1)
        top = jnp.max(scores, -1, keepdims=True)
        weights = jnp.exp2((scores - top) * scale).astype(jnp.bfloat16)
        both = jnp.dot(weights, values, preferred_element_type=jnp.float32)
        summed, total = both[:, :channels], both[:, channels:]
        mean = jnp.mean(summed * summed, -1, keepdims=True)
        normed = summed * lax.rsqrt(mean + EPSILON * (total * total))
        for h in range(some):
            columns = pl.ds((begin + h) * channels, channels)
            out[rows, columns] = (
                normed[h * block : (h + 1) * block] * gain[:, columns]
            ).astype(jnp.bfloat16)


def kernel(
    shards,
    per_span,
    heads,
    q_hbm,
    kv_hbm,
    qt_hbm,
    pt_hbm,
    gahbm,
    table_hbm,
    low_hbm,
    qc_hbm,
    kvc_hbm,
    gath_hbm,
    xq,
    xkv,
    qt,
    pt,
    gain,
    table,
    qc,
    kvc,
    gath,
    out,
    in_sem,
    small_sem,
    own_halo_sem,
    halo_send,
    halo_recv,
    span_send,
    span_recv,
    out_sem,
    hand_sem,
):
    place = lax.axis_index("ctx")
    block = TRANSFORM_BLOCK
    span_rows = per_span * block
    half = per_span * KEEP
    channels = HEAD_CHANNELS

    loads = {}
    for s in range(2):
        loads["kv", s] = pltpu.make_async_copy(
            kv_hbm.at[pl.ds(s * span_rows, span_rows), :],
            xkv.at[s, pl.ds(HALO, span_rows), :],
            in_sem.at[s],
        )
        loads["q", s] = pltpu.make_async_copy(
            q_hbm.at[pl.ds(s * span_rows, span_rows), :],
            xq.at[s, pl.ds(HALO, span_rows), :],
            in_sem.at[2 + s],
        )
    small = [
        pltpu.make_async_copy(source, target, small_sem.at[n])
        for n, (source, target) in enumerate(
            [(pt_hbm, pt), (table_hbm, table), (qt_hbm, qt), (gahbm, gain)]
        )
    ]
    loads["kv", 0].start()
    loads["kv", 1].start()
    for copy in small:
        copy.start()
    loads["q", 0].start()
    loads["q", 1].start()

    barrier = pltpu.get_barrier_semaphore()
    for d in range(1, shards):
        pl.semaphore_signal(
            barrier,
            inc=1,
            device_id={"ctx": lax.rem(place + d, shards)},
            device_id_type=MESH,
        )
    pl.semaphore_wait(barrier, shards - 1)

    def halo_copy(n, s, step):
        source, target = ((kv_hbm, xkv), (q_hbm, xq))[n]
        return pltpu.make_async_remote_copy(
            src_ref=source.at[pl.ds((s + 1) * span_rows - HALO, HALO), :],
            dst_ref=target.at[s, pl.ds(0, HALO), :],
            send_sem=halo_send.at[n, s],
            recv_sem=halo_recv.at[n, s],
            device_id={"ctx": lax.rem(place + step + shards, shards)},
            device_id_type=MESH,
        )

    def own_halo(n):
        source, target = ((kv_hbm, xkv), (q_hbm, xq))[n]
        return pltpu.make_async_copy(
            source.at[pl.ds(span_rows - HALO, HALO), :],
            target.at[1, pl.ds(0, HALO), :],
            own_halo_sem.at[n],
        )

    first = place == 0
    last = place == shards - 1
    for n in range(2):

        @pl.when(jnp.logical_not(last))
        def _():
            halo_copy(n, 0, 1).start()

        @pl.when(jnp.logical_not(first))
        def _():
            halo_copy(n, 1, -1).start()

        @pl.when(last)
        def _():
            own_halo(n).start()

    @pl.when(first)
    def _():
        xkv[0, :HALO, :] = jnp.zeros((HALO, xkv.shape[2]), xkv.dtype)
        xq[0, :HALO, :] = jnp.zeros((HALO, xq.shape[2]), xq.dtype)

    for q in range(shards - 1):

        @pl.when(q < place)
        def _():
            gath[2 * shards - 1 - q] = jnp.zeros(gath.shape[1:], gath.dtype)

    def wait_halo(n):
        @pl.when(jnp.logical_not(first))
        def _():
            halo_copy(n, 0, 1).wait_recv()

        @pl.when(jnp.logical_not(last))
        def _():
            halo_copy(n, 1, -1).wait_recv()

        @pl.when(last)
        def _():
            own_halo(n).wait()

    def conv(source, s, i, taps, g):
        columns = pl.ds(g * channels, channels)
        rows = pl.ds(pl.multiple_of(i * block, block), block + HALO)
        x = source[s, rows, columns].astype(jnp.float32)
        w = taps[:, columns]
        back = pltpu.roll(x, 1, 0)
        newer = w[0:1] * x[HALO:] + w[1:2] * back[HALO:]
        older = w[2:3] * x[HALO // 2 :] + w[3:4] * back[HALO // 2 :]
        older = pltpu.roll(older, 2, 0)[HALO // 2 :]
        return (newer + older).astype(jnp.bfloat16)

    spans = (place, 2 * shards - 1 - place)

    def pair_block(s, i):
        for g in range(2):
            kvc[s * per_span + i, :, g * channels : (g + 1) * channels] = conv(
                xkv, s, i, pt, g
            )
        packed = jnp.dot(
            table[...], kvc[s * per_span + i], preferred_element_type=jnp.float32
        )
        gath[spans[s], pl.ds(pl.multiple_of(i * KEEP, KEEP), KEEP), :] = packed.astype(
            jnp.bfloat16
        )

    def query_block(s, i):
        for h in range(heads):
            qc[s * per_span + i, h] = conv(xq, s, i, qt, h)

    small[0].wait()
    small[1].wait()
    for s in range(2):
        loads["kv", s].wait()
        loop(1, per_span, functools.partial(pair_block, s))

    mate = place + 1 - 2 * lax.rem(place, 2)
    chips = shards // 2

    def peer(d):
        return lax.rem(place + 2 * d, shards)

    def span_copy(s, span, target, part, hop):
        rows = (pl.ds(0, KEEP), pl.ds(KEEP, half - KEEP))[part]
        return pltpu.make_async_remote_copy(
            src_ref=gath.at[span, rows, :],
            dst_ref=gath.at[span, rows, :],
            send_sem=span_send.at[part, s, hop],
            recv_sem=span_recv.at[part, span],
            device_id={"ctx": target},
            device_id_type=MESH,
        )

    def when(condition, act):
        @pl.when(condition)
        def _():
            act()

    def own_copies(part, act):
        for d in range(1, chips):
            target = peer(d)
            other = target + 1 - 2 * lax.rem(target, 2)
            act(span_copy(0, spans[0], target, part, d))
            when(
                target > place,
                lambda: act(span_copy(0, spans[0], other, part, shards + d)),
            )
            when(target < place, lambda: act(span_copy(1, spans[1], target, part, d)))
        act(span_copy(0, spans[0], mate, part, 0))
        when(mate < place, lambda: act(span_copy(1, spans[1], mate, part, 0)))

    def passed_copies(part, d, act):
        source = peer(d)
        upper = 2 * shards - 1 - source

        def both():
            act(span_copy(0, source, mate, part, shards + chips + d))
            act(span_copy(1, upper, mate, part, shards + chips + d))

        when(source > place, both)

    def arrive(s, q, part):
        span = (q, 2 * shards - 1 - q)[s]
        span_copy(s, span, mate, part, 0).wait_recv()

    def pass_on(part):
        for d in range(1, chips):
            source = peer(d)

            def both():
                arrive(0, source, part)
                arrive(1, source, part)

            when(source > place, both)
            passed_copies(part, d, lambda copy: copy.start())

    own_copies(1, lambda copy: copy.start())
    wait_halo(0)
    for s in range(2):
        pair_block(s, 0)
    own_copies(0, lambda copy: copy.start())

    small[2].wait()
    small[3].wait()
    for s in range(2):
        loads["q", s].wait()
        loop(1, per_span, functools.partial(query_block, s))
    wait_halo(1)
    for s in range(2):
        query_block(s, 0)

    block_id = functools.partial(block_of, place, shards, per_span)
    part_rows = 2 * shards * half // FAR_PARTS

    def low_copy(i):
        rows = pl.ds(pl.multiple_of(i * block, block), block)
        return pltpu.make_async_copy(out.at[rows, :], low_hbm.at[rows, :], out_sem.at[i])

    def awaited(s, q):
        passed = jnp.logical_and(lax.rem(q, 2) == lax.rem(place, 2), q > place)
        return jnp.logical_and(jnp.logical_not(passed), (q != place) if s == 0 else (q > place))

    def needed_parts(index):
        return (block_id(index) * KEEP + part_rows - 1) // part_rows

    lower_spans = needed_parts(per_span - 1) * (part_rows // half)

    def await_spans(s, low, high):
        for q in range(shards):
            wanted = jnp.logical_and(q >= low, q < high)

            @pl.when(jnp.logical_and(wanted, awaited(s, q)))
            def _():
                for part in range(2):
                    arrive(s, q, part)

    handed = [
        pltpu.make_async_copy(source, target, hand_sem.at[n])
        for n, (source, target) in enumerate(
            [
                (qc.at[pl.ds(per_span, per_span)], qc_hbm),
                (kvc.at[pl.ds(per_span, per_span)], kvc_hbm),
                (gath, gath_hbm),
            ]
        )
    ]
    handed[0].start()
    handed[1].start()

    early = lower_spans > place - lax.rem(place, 2) + 2

    @pl.when(early)
    def _():
        pass_on(1)
        pass_on(0)

    await_spans(0, 0, lower_spans)

    def step(index):
        @pl.when(jnp.logical_and(index == min(1, per_span - 1), jnp.logical_not(early)))
        def _():
            pass_on(1)
            pass_on(0)

        @pl.when(index == per_span - 1)
        def _():
            await_spans(0, lower_spans, shards)
            await_spans(1, 0, shards)
            handed[2].start()

        attend_block(
            qc, kvc, gath, gain, out, index, block_id(index), part_rows, 1, FAR_PARTS // 2
        )
        low_copy(index).start()

    loop(0, per_span, step)
    loop(0, per_span, lambda index: low_copy(index).wait())
    for copy in handed:
        copy.wait()

    for n in range(2):

        @pl.when(jnp.logical_not(last))
        def _():
            halo_copy(n, 0, 1).wait_send()

        @pl.when(jnp.logical_not(first))
        def _():
            halo_copy(n, 1, -1).wait_send()

    for part in range(2):
        own_copies(part, lambda copy: copy.wait_send())
        for d in range(1, chips):
            passed_copies(part, d, lambda copy: copy.wait_send())


def upper_kernel(
    shards,
    per_span,
    heads,
    low_hbm,
    qc_hbm,
    kvc_hbm,
    gath_hbm,
    gain_hbm,
    out_hbm,
    qc,
    kvc,
    gath,
    gain,
    out,
    low,
    in_sem,
    q_sem,
    out_sem,
    low_sem,
):
    place = lax.axis_index("ctx")
    block = TRANSFORM_BLOCK
    span_rows = per_span * block
    part_rows = 2 * shards * per_span * KEEP // FAR_PARTS

    loads = [
        pltpu.make_async_copy(source, target, in_sem.at[n])
        for n, (source, target) in enumerate(
            [(gath_hbm, gath), (kvc_hbm, kvc), (gain_hbm, gain)]
        )
    ]

    def query_load(i):
        return pltpu.make_async_copy(qc_hbm.at[i], qc.at[i], q_sem.at[i])

    query_load(0).start()
    for copy in loads:
        copy.start()
    loop(1, per_span, lambda i: query_load(i).start())
    low_load = pltpu.make_async_copy(low_hbm, low, low_sem.at[0])
    low_store = pltpu.make_async_copy(
        low, out_hbm.at[pl.ds(0, span_rows), :], low_sem.at[1]
    )
    low_load.start()

    def out_copy(i):
        rows = pl.ds(pl.multiple_of(i * block, block), block)
        target = pl.ds(pl.multiple_of(span_rows + i * block, block), block)
        return pltpu.make_async_copy(
            out.at[rows, :], out_hbm.at[target, :], out_sem.at[i]
        )

    for copy in loads:
        copy.wait()

    def step(i):
        query_load(i).wait()
        block_id = block_of(place, shards, per_span, per_span + i)
        attend_block(
            qc, kvc, gath, gain, out, i, block_id, part_rows, FAR_PARTS // 2, FAR_PARTS
        )
        out_copy(i).start()

        @pl.when(i == 0)
        def _():
            low_load.wait()
            low_store.start()

    loop(0, per_span, step)
    loop(0, per_span, lambda i: out_copy(i).wait())
    low_store.wait()


def attention(queries, pairs, query_taps, pair_taps, out_gain, shards):
    rows, columns = queries.shape
    span_rows = rows // 2
    per_span = span_rows // TRANSFORM_BLOCK
    heads = columns // HEAD_CHANNELS
    half = per_span * KEEP
    blocks = 2 * per_span
    bf16, f32 = jnp.bfloat16, jnp.float32
    width = 2 * HEAD_CHANNELS
    hbm = pl.BlockSpec(memory_space=pltpu.HBM)
    dma = pltpu.SemaphoreType.DMA
    gain = out_gain.reshape(1, columns)
    half_q = (per_span, heads, TRANSFORM_BLOCK, HEAD_CHANNELS)
    half_kv = (per_span, TRANSFORM_BLOCK, width)
    all_packed = (2 * shards, half, width)
    handed = pl.pallas_call(
        functools.partial(kernel, shards, per_span, heads),
        out_shape=[
            jax.ShapeDtypeStruct((span_rows, columns), bf16),
            jax.ShapeDtypeStruct(half_q, bf16),
            jax.ShapeDtypeStruct(half_kv, bf16),
            jax.ShapeDtypeStruct(all_packed, bf16),
        ],
        in_specs=[hbm] * 6,
        out_specs=[hbm] * 4,
        scratch_shapes=[
            pltpu.VMEM((2, HALO + span_rows, columns), bf16),
            pltpu.VMEM((2, HALO + span_rows, width), bf16),
            pltpu.VMEM((TAPS, columns), f32),
            pltpu.VMEM((TAPS, width), f32),
            pltpu.VMEM((1, columns), f32),
            pltpu.VMEM((KEEP, TRANSFORM_BLOCK), bf16),
            pltpu.VMEM((blocks, heads, TRANSFORM_BLOCK, HEAD_CHANNELS), bf16),
            pltpu.VMEM((blocks, TRANSFORM_BLOCK, width), bf16),
            pltpu.VMEM(all_packed, bf16),
            pltpu.VMEM((span_rows, columns), bf16),
            dma((4,)),
            dma((4,)),
            dma((2,)),
            dma((2, 2)),
            dma((2, 2)),
            dma((2, 2, 2 * shards)),
            dma((2, 2 * shards)),
            dma((per_span,)),
            dma((3,)),
        ],
        compiler_params=pltpu.CompilerParams(
            collective_id=0, has_side_effects=True, vmem_limit_bytes=62 * 1024 * 1024
        ),
        name="exchange_and_lower",
    )(
        queries,
        pairs,
        query_taps,
        pair_taps,
        gain,
        jnp.asarray(dct_table()),
    )
    return pl.pallas_call(
        functools.partial(upper_kernel, shards, per_span, heads),
        out_shape=jax.ShapeDtypeStruct((rows, columns), bf16),
        in_specs=[hbm] * 5,
        out_specs=hbm,
        scratch_shapes=[
            pltpu.VMEM(half_q, bf16),
            pltpu.VMEM(half_kv, bf16),
            pltpu.VMEM(all_packed, bf16),
            pltpu.VMEM((1, columns), f32),
            pltpu.VMEM((span_rows, columns), bf16),
            pltpu.VMEM((span_rows, columns), bf16),
            dma((3,)),
            dma((per_span,)),
            dma((per_span,)),
            dma((2,)),
        ],
        compiler_params=pltpu.CompilerParams(vmem_limit_bytes=62 * 1024 * 1024),
        name="upper",
    )(*handed, gain)


def from_partner(block, axis, apart):
    count = lax.axis_size(axis)
    route = []
    for low in range(count):
        high = low | 1 << apart
        if high != low and high < count:
            route += [(low, high), (high, low)]
    return lax.ppermute(block, axis, route)


def per_device(queries, keys_values, query_taps, pair_taps, out_gain):
    member = lax.axis_index("mp")
    width = keys_values.shape[1]
    rounds = (2 * HEAD_CHANNELS // width).bit_length() - 1

    def join(mine, bit):
        other = from_partner(mine, "mp", bit)
        lower = member // 2**bit % 2 == 0
        return jnp.where(
            lower, jnp.concatenate([mine, other], 1), jnp.concatenate([other, mine], 1)
        )

    for bit in range(rounds):
        keys_values = join(keys_values, bit)
        pair_taps = join(pair_taps, bit)
    return attention(
        queries, keys_values, query_taps, pair_taps, out_gain, lax.axis_size("ctx")
    )


def solution(mesh):
    in_specs = (P("ctx", "mp"), P("ctx", "mp"), P(None, "mp"), P(None, "mp"), P("mp"))
    out_specs = P("ctx", "mp")
    return jax.shard_map(
        per_device, mesh=mesh, in_specs=in_specs, out_specs=out_specs, check_vma=False
    )
```

```python
import functools
import math

import jax
import jax.numpy as jnp
import numpy as np
from jax import lax
from jax.experimental import pallas as pl
from jax.experimental.pallas import tpu as pltpu
from jax.sharding import PartitionSpec as P

HEAD_CHANNELS = 128
TAPS = 4
TRANSFORM_BLOCK = 128
KEEP = 16
HALO = 16
FAR_PARTS = 4

NEGATIVE = -1e30
EPSILON = 1e-06
MESH = pl.DeviceIdType.MESH


def dct_table():
    frequency = np.arange(KEEP, dtype=np.float32)[:, None]
    offset = np.arange(TRANSFORM_BLOCK, dtype=np.float32)[None, :]
    angle = np.float32(math.pi) * (offset + np.float32(0.5)) * frequency
    table = np.cos(angle / np.float32(TRANSFORM_BLOCK)) * np.float32(
        math.sqrt(2.0 / TRANSFORM_BLOCK)
    )
    table = np.where(frequency == 0.0, table * np.float32(math.sqrt(0.5)), table)
    return table.astype(jnp.bfloat16)


def nt_dot(left, right):
    return lax.dot_general(
        left, right, (((1,), (1,)), ((), ())), preferred_element_type=jnp.float32
    )


def loop(low, high, body):
    def step(i, carry):
        body(i)
        return carry

    lax.fori_loop(low, high, step, 0)


def block_of(place, shards, per_span, index):
    upper = index // per_span
    span = place + upper * (2 * shards - 1 - 2 * place)
    return span * per_span + lax.rem(index, per_span)


def attend_block(qc, kvc, gath, gain, out, index, block_id, part_rows, least, most):
    needed = (block_id * KEEP + part_rows - 1) // part_rows
    for parts in range(least, most + 1):
        fits = needed <= least if parts == least else needed == parts

        @pl.when(fits)
        def _():
            attend(qc, kvc, gath, gain, out, index, block_id, part_rows, parts)


def attend(qc, kvc, gath, gain, out, index, block_id, part_rows, parts):
    block, channels = TRANSFORM_BLOCK, HEAD_CHANNELS
    heads, half = qc.shape[1], gath.shape[1]
    scale = math.log2(math.e) / math.sqrt(channels)
    row_id = lax.broadcasted_iota(jnp.int32, (block, block), 0)
    column_id = lax.broadcasted_iota(jnp.int32, (block, block), 1)
    far_rows = parts * part_rows
    near = kvc[index]
    far = gath[: far_rows // half].reshape(far_rows, 2 * channels)
    near_bias = jnp.where(row_id >= column_id, 0.0, NEGATIVE)
    far_ids = lax.broadcasted_iota(jnp.int32, (1, part_rows), 1)
    far_bias = jnp.where(
        far_ids + (far_rows - part_rows) < block_id * KEEP, 0.0, NEGATIVE
    )
    keys = jnp.concatenate([near[:, :channels], far[:, :channels]], 0)
    values = jnp.concatenate([near[:, channels:], far[:, channels:]], 0)
    values = jnp.concatenate([values, jnp.ones_like(values)], 1)
    rows = pl.ds(pl.multiple_of(index * block, block), block)
    some = heads
    for begin in range(0, heads, some):
        query = qc[index, begin : begin + some].reshape(some * block, channels)
        scores = nt_dot(query, keys)
        near_scores = (
            scores[:, :block].reshape(some, block, block) + near_bias[None]
        ).reshape(some * block, block)
        pieces = [near_scores, scores[:, block + far_rows - part_rows :] + far_bias]
        if parts > 1:
            pieces.insert(1, scores[:, block : block + far_rows - part_rows])
        scores = jnp.concatenate(pieces, 1)
        top = jnp.max(scores, -1, keepdims=True)
        weights = jnp.exp2((scores - top) * scale).astype(jnp.bfloat16)
        both = jnp.dot(weights, values, preferred_element_type=jnp.float32)
        summed, total = both[:, :channels], both[:, channels:]
        mean = jnp.mean(summed * summed, -1, keepdims=True)
        normed = summed * lax.rsqrt(mean + EPSILON * (total * total))
        for h in range(some):
            columns = pl.ds((begin + h) * channels, channels)
            out[rows, columns] = (
                normed[h * block : (h + 1) * block] * gain[:, columns]
            ).astype(jnp.bfloat16)


def kernel(
    shards,
    per_span,
    heads,
    q_hbm,
    kv_hbm,
    qt_hbm,
    pt_hbm,
    gahbm,
    table_hbm,
    low_hbm,
    qc_hbm,
    kvc_hbm,
    gath_hbm,
    xq,
    xkv,
    qt,
    pt,
    gain,
    table,
    qc,
    kvc,
    gath,
    out,
    in_sem,
    small_sem,
    own_halo_sem,
    halo_send,
    halo_recv,
    span_send,
    span_recv,
    out_sem,
    hand_sem,
):
    place = lax.axis_index("ctx")
    block = TRANSFORM_BLOCK
    span_rows = per_span * block
    half = per_span * KEEP
    channels = HEAD_CHANNELS

    loads = {}
    for s in range(2):
        loads["kv", s] = pltpu.make_async_copy(
            kv_hbm.at[pl.ds(s * span_rows, span_rows), :],
            xkv.at[s, pl.ds(HALO, span_rows), :],
            in_sem.at[s],
        )
        loads["q", s] = pltpu.make_async_copy(
            q_hbm.at[pl.ds(s * span_rows, span_rows), :],
            xq.at[s, pl.ds(HALO, span_rows), :],
            in_sem.at[2 + s],
        )
    small = [
        pltpu.make_async_copy(source, target, small_sem.at[n])
        for n, (source, target) in enumerate(
            [(pt_hbm, pt), (table_hbm, table), (qt_hbm, qt), (gahbm, gain)]
        )
    ]
    loads["kv", 0].start()
    loads["kv", 1].start()
    for copy in small:
        copy.start()
    loads["q", 0].start()
    loads["q", 1].start()

    barrier = pltpu.get_barrier_semaphore()
    for d in range(1, shards):
        pl.semaphore_signal(
            barrier,
            inc=1,
            device_id={"ctx": lax.rem(place + d, shards)},
            device_id_type=MESH,
        )
    pl.semaphore_wait(barrier, shards - 1)

    def halo_copy(n, s, step):
        source, target = ((kv_hbm, xkv), (q_hbm, xq))[n]
        return pltpu.make_async_remote_copy(
            src_ref=source.at[pl.ds((s + 1) * span_rows - HALO, HALO), :],
            dst_ref=target.at[s, pl.ds(0, HALO), :],
            send_sem=halo_send.at[n, s],
            recv_sem=halo_recv.at[n, s],
            device_id={"ctx": lax.rem(place + step + shards, shards)},
            device_id_type=MESH,
        )

    def own_halo(n):
        source, target = ((kv_hbm, xkv), (q_hbm, xq))[n]
        return pltpu.make_async_copy(
            source.at[pl.ds(span_rows - HALO, HALO), :],
            target.at[1, pl.ds(0, HALO), :],
            own_halo_sem.at[n],
        )

    first = place == 0
    last = place == shards - 1
    for n in range(2):

        @pl.when(jnp.logical_not(last))
        def _():
            halo_copy(n, 0, 1).start()

        @pl.when(jnp.logical_not(first))
        def _():
            halo_copy(n, 1, -1).start()

        @pl.when(last)
        def _():
            own_halo(n).start()

    @pl.when(first)
    def _():
        xkv[0, :HALO, :] = jnp.zeros((HALO, xkv.shape[2]), xkv.dtype)
        xq[0, :HALO, :] = jnp.zeros((HALO, xq.shape[2]), xq.dtype)

    for q in range(shards - 1):

        @pl.when(q < place)
        def _():
            gath[2 * shards - 1 - q] = jnp.zeros(gath.shape[1:], gath.dtype)

    def wait_halo(n):
        @pl.when(jnp.logical_not(first))
        def _():
            halo_copy(n, 0, 1).wait_recv()

        @pl.when(jnp.logical_not(last))
        def _():
            halo_copy(n, 1, -1).wait_recv()

        @pl.when(last)
        def _():
            own_halo(n).wait()

    def conv(source, s, i, taps, g):
        columns = pl.ds(g * channels, channels)
        rows = pl.ds(pl.multiple_of(i * block, block), block + HALO)
        x = source[s, rows, columns].astype(jnp.float32)
        w = taps[:, columns]
        back = pltpu.roll(x, 1, 0)
        newer = w[0:1] * x[HALO:] + w[1:2] * back[HALO:]
        older = w[2:3] * x[HALO // 2 :] + w[3:4] * back[HALO // 2 :]
        older = pltpu.roll(older, 2, 0)[HALO // 2 :]
        return (newer + older).astype(jnp.bfloat16)

    spans = (place, 2 * shards - 1 - place)

    def pair_block(s, i):
        for g in range(2):
            kvc[s * per_span + i, :, g * channels : (g + 1) * channels] = conv(
                xkv, s, i, pt, g
            )
        packed = jnp.dot(
            table[...], kvc[s * per_span + i], preferred_element_type=jnp.float32
        )
        gath[spans[s], pl.ds(pl.multiple_of(i * KEEP, KEEP), KEEP), :] = packed.astype(
            jnp.bfloat16
        )

    def query_block(s, i):
        for h in range(heads):
            qc[s * per_span + i, h] = conv(xq, s, i, qt, h)

    small[0].wait()
    small[1].wait()
    for s in range(2):
        loads["kv", s].wait()
        loop(1, per_span, functools.partial(pair_block, s))

    mate = place + 1 - 2 * lax.rem(place, 2)
    chips = shards // 2

    def peer(d):
        return lax.rem(place + 2 * d, shards)

    def span_copy(s, span, target, part, hop):
        rows = (pl.ds(0, KEEP), pl.ds(KEEP, half - KEEP))[part]
        return pltpu.make_async_remote_copy(
            src_ref=gath.at[span, rows, :],
            dst_ref=gath.at[span, rows, :],
            send_sem=span_send.at[part, s, hop],
            recv_sem=span_recv.at[part, span],
            device_id={"ctx": target},
            device_id_type=MESH,
        )

    def when(condition, act):
        @pl.when(condition)
        def _():
            act()

    def own_copies(part, act):
        for d in range(1, chips):
            target = peer(d)
            other = target + 1 - 2 * lax.rem(target, 2)
            act(span_copy(0, spans[0], target, part, d))
            when(
                target > place,
                lambda: act(span_copy(0, spans[0], other, part, shards + d)),
            )
            when(target < place, lambda: act(span_copy(1, spans[1], target, part, d)))
        act(span_copy(0, spans[0], mate, part, 0))
        when(mate < place, lambda: act(span_copy(1, spans[1], mate, part, 0)))

    def passed_copies(part, d, act):
        source = peer(d)
        upper = 2 * shards - 1 - source

        def both():
            act(span_copy(0, source, mate, part, shards + chips + d))
            act(span_copy(1, upper, mate, part, shards + chips + d))

        when(source > place, both)

    def arrive(s, q, part):
        span = (q, 2 * shards - 1 - q)[s]
        span_copy(s, span, mate, part, 0).wait_recv()

    def pass_on(part):
        for d in range(1, chips):
            source = peer(d)

            def both():
                arrive(0, source, part)
                arrive(1, source, part)

            when(source > place, both)
            passed_copies(part, d, lambda copy: copy.start())

    own_copies(1, lambda copy: copy.start())
    wait_halo(0)
    for s in range(2):
        pair_block(s, 0)
    own_copies(0, lambda copy: copy.start())

    small[2].wait()
    small[3].wait()
    for s in range(2):
        loads["q", s].wait()
        loop(1, per_span, functools.partial(query_block, s))
    wait_halo(1)
    for s in range(2):
        query_block(s, 0)

    block_id = functools.partial(block_of, place, shards, per_span)
    part_rows = 2 * shards * half // FAR_PARTS

    def low_copy(i):
        rows = pl.ds(pl.multiple_of(i * block, block), block)
        return pltpu.make_async_copy(out.at[rows, :], low_hbm.at[rows, :], out_sem.at[i])

    def awaited(s, q):
        passed = jnp.logical_and(lax.rem(q, 2) == lax.rem(place, 2), q > place)
        return jnp.logical_and(jnp.logical_not(passed), (q != place) if s == 0 else (q > place))

    def needed_parts(index):
        return (block_id(index) * KEEP + part_rows - 1) // part_rows

    lower_spans = needed_parts(per_span - 1) * (part_rows // half)

    def await_spans(s, low, high):
        for q in range(shards):
            wanted = jnp.logical_and(q >= low, q < high)

            @pl.when(jnp.logical_and(wanted, awaited(s, q)))
            def _():
                for part in range(2):
                    arrive(s, q, part)

    handed = [
        pltpu.make_async_copy(source, target, hand_sem.at[n])
        for n, (source, target) in enumerate(
            [
                (qc.at[pl.ds(per_span, per_span)], qc_hbm),
                (kvc.at[pl.ds(per_span, per_span)], kvc_hbm),
                (gath, gath_hbm),
            ]
        )
    ]
    handed[0].start()
    handed[1].start()

    early = lower_spans > place - lax.rem(place, 2) + 2

    @pl.when(early)
    def _():
        pass_on(1)
        pass_on(0)

    await_spans(0, 0, lower_spans)

    def step(index):
        @pl.when(jnp.logical_and(index == min(1, per_span - 1), jnp.logical_not(early)))
        def _():
            pass_on(1)
            pass_on(0)

        @pl.when(index == per_span - 1)
        def _():
            await_spans(0, lower_spans, shards)
            await_spans(1, 0, shards)
            handed[2].start()

        attend_block(
            qc, kvc, gath, gain, out, index, block_id(index), part_rows, 1, FAR_PARTS // 2
        )
        low_copy(index).start()

    loop(0, per_span, step)
    loop(0, per_span, lambda index: low_copy(index).wait())
    for copy in handed:
        copy.wait()

    for n in range(2):

        @pl.when(jnp.logical_not(last))
        def _():
            halo_copy(n, 0, 1).wait_send()

        @pl.when(jnp.logical_not(first))
        def _():
            halo_copy(n, 1, -1).wait_send()

    for part in range(2):
        own_copies(part, lambda copy: copy.wait_send())
        for d in range(1, chips):
            passed_copies(part, d, lambda copy: copy.wait_send())


def upper_kernel(
    shards,
    per_span,
    heads,
    low_hbm,
    qc_hbm,
    kvc_hbm,
    gath_hbm,
    gain_hbm,
    out_hbm,
    qc,
    kvc,
    gath,
    gain,
    out,
    low,
    in_sem,
    q_sem,
    out_sem,
    low_sem,
):
    place = lax.axis_index("ctx")
    block = TRANSFORM_BLOCK
    span_rows = per_span * block
    part_rows = 2 * shards * per_span * KEEP // FAR_PARTS

    loads = [
        pltpu.make_async_copy(source, target, in_sem.at[n])
        for n, (source, target) in enumerate(
            [(gath_hbm, gath), (kvc_hbm, kvc), (gain_hbm, gain)]
        )
    ]

    def query_load(i):
        return pltpu.make_async_copy(qc_hbm.at[i], qc.at[i], q_sem.at[i])

    query_load(0).start()
    for copy in loads:
        copy.start()
    loop(1, per_span, lambda i: query_load(i).start())
    low_load = pltpu.make_async_copy(low_hbm, low, low_sem.at[0])
    low_store = pltpu.make_async_copy(
        low, out_hbm.at[pl.ds(0, span_rows), :], low_sem.at[1]
    )
    low_load.start()

    def out_copy(i):
        rows = pl.ds(pl.multiple_of(i * block, block), block)
        target = pl.ds(pl.multiple_of(span_rows + i * block, block), block)
        return pltpu.make_async_copy(
            out.at[rows, :], out_hbm.at[target, :], out_sem.at[i]
        )

    for copy in loads:
        copy.wait()

    def step(i):
        query_load(i).wait()
        block_id = block_of(place, shards, per_span, per_span + i)
        attend_block(
            qc, kvc, gath, gain, out, i, block_id, part_rows, FAR_PARTS // 2, FAR_PARTS
        )
        out_copy(i).start()

        @pl.when(i == 0)
        def _():
            low_load.wait()
            low_store.start()

    loop(0, per_span, step)
    loop(0, per_span, lambda i: out_copy(i).wait())
    low_store.wait()


def attention(queries, pairs, query_taps, pair_taps, out_gain, shards):
    rows, columns = queries.shape
    span_rows = rows // 2
    per_span = span_rows // TRANSFORM_BLOCK
    heads = columns // HEAD_CHANNELS
    half = per_span * KEEP
    blocks = 2 * per_span
    bf16, f32 = jnp.bfloat16, jnp.float32
    width = 2 * HEAD_CHANNELS
    hbm = pl.BlockSpec(memory_space=pltpu.HBM)
    dma = pltpu.SemaphoreType.DMA
    gain = out_gain.reshape(1, columns)
    half_q = (per_span, heads, TRANSFORM_BLOCK, HEAD_CHANNELS)
    half_kv = (per_span, TRANSFORM_BLOCK, width)
    all_packed = (2 * shards, half, width)
    handed = pl.pallas_call(
        functools.partial(kernel, shards, per_span, heads),
        out_shape=[
            jax.ShapeDtypeStruct((span_rows, columns), bf16),
            jax.ShapeDtypeStruct(half_q, bf16),
            jax.ShapeDtypeStruct(half_kv, bf16),
            jax.ShapeDtypeStruct(all_packed, bf16),
        ],
        in_specs=[hbm] * 6,
        out_specs=[hbm] * 4,
        scratch_shapes=[
            pltpu.VMEM((2, HALO + span_rows, columns), bf16),
            pltpu.VMEM((2, HALO + span_rows, width), bf16),
            pltpu.VMEM((TAPS, columns), f32),
            pltpu.VMEM((TAPS, width), f32),
            pltpu.VMEM((1, columns), f32),
            pltpu.VMEM((KEEP, TRANSFORM_BLOCK), bf16),
            pltpu.VMEM((blocks, heads, TRANSFORM_BLOCK, HEAD_CHANNELS), bf16),
            pltpu.VMEM((blocks, TRANSFORM_BLOCK, width), bf16),
            pltpu.VMEM(all_packed, bf16),
            pltpu.VMEM((span_rows, columns), bf16),
            dma((4,)),
            dma((4,)),
            dma((2,)),
            dma((2, 2)),
            dma((2, 2)),
            dma((2, 2, 2 * shards)),
            dma((2, 2 * shards)),
            dma((per_span,)),
            dma((3,)),
        ],
        compiler_params=pltpu.CompilerParams(
            collective_id=0, has_side_effects=True, vmem_limit_bytes=62 * 1024 * 1024
        ),
        name="exchange_and_lower",
    )(
        queries,
        pairs,
        query_taps,
        pair_taps,
        gain,
        jnp.asarray(dct_table()),
    )
    return pl.pallas_call(
        functools.partial(upper_kernel, shards, per_span, heads),
        out_shape=jax.ShapeDtypeStruct((rows, columns), bf16),
        in_specs=[hbm] * 5,
        out_specs=hbm,
        scratch_shapes=[
            pltpu.VMEM(half_q, bf16),
            pltpu.VMEM(half_kv, bf16),
            pltpu.VMEM(all_packed, bf16),
            pltpu.VMEM((1, columns), f32),
            pltpu.VMEM((span_rows, columns), bf16),
            pltpu.VMEM((span_rows, columns), bf16),
            dma((3,)),
            dma((per_span,)),
            dma((per_span,)),
            dma((2,)),
        ],
        compiler_params=pltpu.CompilerParams(vmem_limit_bytes=62 * 1024 * 1024),
        name="upper",
    )(*handed, gain)


def from_partner(block, axis, apart):
    count = lax.axis_size(axis)
    route = []
    for low in range(count):
        high = low | 1 << apart
        if high != low and high < count:
            route += [(low, high), (high, low)]
    return lax.ppermute(block, axis, route)


def per_device(queries, keys_values, query_taps, pair_taps, out_gain):
    member = lax.axis_index("mp")
    width = keys_values.shape[1]
    rounds = (2 * HEAD_CHANNELS // width).bit_length() - 1

    def join(mine, bit):
        other = from_partner(mine, "mp", bit)
        lower = member // 2**bit % 2 == 0
        return jnp.where(
            lower, jnp.concatenate([mine, other], 1), jnp.concatenate([other, mine], 1)
        )

    for bit in range(rounds):
        keys_values = join(keys_values, bit)
        pair_taps = join(pair_taps, bit)
    return attention(
        queries, keys_values, query_taps, pair_taps, out_gain, lax.axis_size("ctx")
    )


def solution(mesh):
    in_specs = (P("ctx", "mp"), P("ctx", "mp"), P(None, "mp"), P(None, "mp"), P("mp"))
    out_specs = P("ctx", "mp")
    return jax.shard_map(
        per_device, mesh=mesh, in_specs=in_specs, out_specs=out_specs, check_vma=False
    )
```

```python
import functools
import math

import jax
import jax.numpy as jnp
import numpy as np
from jax import lax
from jax.experimental import pallas as pl
from jax.experimental.pallas import tpu as pltpu
from jax.sharding import PartitionSpec as P

HEAD_CHANNELS = 128
TAPS = 4
TRANSFORM_BLOCK = 128
KEEP = 16
HALO = 16
FAR_PARTS = 4

NEGATIVE = -1e30
EPSILON = 1e-06
MESH = pl.DeviceIdType.MESH


def dct_table():
    frequency = np.arange(KEEP, dtype=np.float32)[:, None]
    offset = np.arange(TRANSFORM_BLOCK, dtype=np.float32)[None, :]
    angle = np.float32(math.pi) * (offset + np.float32(0.5)) * frequency
    table = np.cos(angle / np.float32(TRANSFORM_BLOCK)) * np.float32(
        math.sqrt(2.0 / TRANSFORM_BLOCK)
    )
    table = np.where(frequency == 0.0, table * np.float32(math.sqrt(0.5)), table)
    return table.astype(jnp.bfloat16)


def nt_dot(left, right):
    return lax.dot_general(
        left, right, (((1,), (1,)), ((), ())), preferred_element_type=jnp.float32
    )


def loop(low, high, body):
    def step(i, carry):
        body(i)
        return carry

    lax.fori_loop(low, high, step, 0)


def block_of(place, shards, per_span, index):
    upper = index // per_span
    span = place + upper * (2 * shards - 1 - 2 * place)
    return span * per_span + lax.rem(index, per_span)


def attend_blocks(qc, kvc, gath, gain, out, index, count, block_id, part_rows, least, most):
    needed = ((block_id + count - 1) * KEEP + part_rows - 1) // part_rows
    for parts in range(least, most + 1):
        fits = needed <= least if parts == least else needed == parts

        @pl.when(fits)
        def _():
            attend(qc, kvc, gath, gain, out, index, count, block_id, part_rows, parts)


def attend(qc, kvc, gath, gain, out, index, count, block_id, part_rows, parts):
    block, channels = TRANSFORM_BLOCK, HEAD_CHANNELS
    heads, half = qc.shape[1], gath.shape[1]
    scale = math.log2(math.e) / math.sqrt(channels)
    row_id = lax.broadcasted_iota(jnp.int32, (block, block), 0)
    column_id = lax.broadcasted_iota(jnp.int32, (block, block), 1)
    near_bias = jnp.where(row_id >= column_id, 0.0, NEGATIVE)
    far_rows = parts * part_rows
    open_rows = block + far_rows - part_rows
    far = gath[: far_rows // half].reshape(far_rows, 2 * channels)
    far_ids = lax.broadcasted_iota(jnp.int32, (1, part_rows), 1) + (far_rows - part_rows)
    some = min(heads, 2)
    for step in range(count):
        near = kvc[index + step]
        far_bias = jnp.where(far_ids < (block_id + step) * KEEP, 0.0, NEGATIVE)
        keys = jnp.concatenate([near[:, :channels], far[:, :channels]], 0)
        values = jnp.concatenate([near[:, channels:], far[:, channels:]], 0)
        values = jnp.concatenate([values, jnp.ones_like(values)], 1)
        rows = pl.ds(pl.multiple_of((index + step) * block, block), block)
        for begin in range(0, heads, some):
            query = qc[index + step, begin : begin + some].reshape(some * block, channels)
            scores = nt_dot(query, keys)
            near_scores = (
                scores[:, :block].reshape(some, block, block) + near_bias[None]
            ).reshape(some * block, block)
            pieces = [near_scores, scores[:, open_rows:] + far_bias]
            if parts > 1:
                pieces.insert(1, scores[:, block:open_rows])
            scores = jnp.concatenate(pieces, 1)
            top = jnp.max(scores, -1, keepdims=True)
            weights = jnp.exp2((scores - top) * scale).astype(jnp.bfloat16)
            both = jnp.dot(weights, values, preferred_element_type=jnp.float32)
            summed, total = both[:, :channels], both[:, channels:]
            mean = jnp.mean(summed * summed, -1, keepdims=True)
            normed = summed * lax.rsqrt(mean + EPSILON * (total * total))
            for h in range(some):
                columns = pl.ds((begin + h) * channels, channels)
                out[rows, columns] = (
                    normed[h * block : (h + 1) * block] * gain[:, columns]
                ).astype(jnp.bfloat16)


def kernel(
    shards,
    per_span,
    heads,
    q_hbm,
    kv_hbm,
    qt_hbm,
    pt_hbm,
    gahbm,
    table_hbm,
    low_hbm,
    qc_hbm,
    kvc_hbm,
    gath_hbm,
    xq,
    xkv,
    qt,
    pt,
    gain,
    table,
    qc,
    kvc,
    gath,
    out,
    in_sem,
    small_sem,
    own_halo_sem,
    halo_send,
    halo_recv,
    span_send,
    span_recv,
    out_sem,
    hand_sem,
):
    place = lax.axis_index("ctx")
    block = TRANSFORM_BLOCK
    span_rows = per_span * block
    half = per_span * KEEP
    channels = HEAD_CHANNELS

    loads = {}
    for s in range(2):
        loads["kv", s] = pltpu.make_async_copy(
            kv_hbm.at[pl.ds(s * span_rows, span_rows), :],
            xkv.at[s, pl.ds(HALO, span_rows), :],
            in_sem.at[s],
        )
        loads["q", s] = pltpu.make_async_copy(
            q_hbm.at[pl.ds(s * span_rows, span_rows), :],
            xq.at[s, pl.ds(HALO, span_rows), :],
            in_sem.at[2 + s],
        )
    small = [
        pltpu.make_async_copy(source, target, small_sem.at[n])
        for n, (source, target) in enumerate(
            [(pt_hbm, pt), (table_hbm, table), (qt_hbm, qt), (gahbm, gain)]
        )
    ]
    loads["kv", 0].start()
    loads["kv", 1].start()
    for copy in small:
        copy.start()
    loads["q", 0].start()
    loads["q", 1].start()

    barrier = pltpu.get_barrier_semaphore()
    for d in range(1, shards):
        pl.semaphore_signal(
            barrier,
            inc=1,
            device_id={"ctx": lax.rem(place + d, shards)},
            device_id_type=MESH,
        )
    pl.semaphore_wait(barrier, shards - 1)

    def halo_copy(n, s, step):
        source, target = ((kv_hbm, xkv), (q_hbm, xq))[n]
        return pltpu.make_async_remote_copy(
            src_ref=source.at[pl.ds((s + 1) * span_rows - HALO, HALO), :],
            dst_ref=target.at[s, pl.ds(0, HALO), :],
            send_sem=halo_send.at[n, s],
            recv_sem=halo_recv.at[n, s],
            device_id={"ctx": lax.rem(place + step + shards, shards)},
            device_id_type=MESH,
        )

    def own_halo(n):
        source, target = ((kv_hbm, xkv), (q_hbm, xq))[n]
        return pltpu.make_async_copy(
            source.at[pl.ds(span_rows - HALO, HALO), :],
            target.at[1, pl.ds(0, HALO), :],
            own_halo_sem.at[n],
        )

    first = place == 0
    last = place == shards - 1
    for n in range(2):

        @pl.when(jnp.logical_not(last))
        def _():
            halo_copy(n, 0, 1).start()

        @pl.when(jnp.logical_not(first))
        def _():
            halo_copy(n, 1, -1).start()

        @pl.when(last)
        def _():
            own_halo(n).start()

    @pl.when(first)
    def _():
        xkv[0, :HALO, :] = jnp.zeros((HALO, xkv.shape[2]), xkv.dtype)
        xq[0, :HALO, :] = jnp.zeros((HALO, xq.shape[2]), xq.dtype)

    for q in range(shards - 1):

        @pl.when(q < place)
        def _():
            gath[2 * shards - 1 - q] = jnp.zeros(gath.shape[1:], gath.dtype)

    def wait_halo(n):
        @pl.when(jnp.logical_not(first))
        def _():
            halo_copy(n, 0, 1).wait_recv()

        @pl.when(jnp.logical_not(last))
        def _():
            halo_copy(n, 1, -1).wait_recv()

        @pl.when(last)
        def _():
            own_halo(n).wait()

    def conv(source, s, i, taps, g):
        columns = pl.ds(g * channels, channels)
        rows = pl.ds(pl.multiple_of(i * block, block), block + HALO)
        x = source[s, rows, columns].astype(jnp.float32)
        w = taps[:, columns]
        back = pltpu.roll(x, 1, 0)
        newer = w[0:1] * x[HALO:] + w[1:2] * back[HALO:]
        older = w[2:3] * x[HALO // 2 :] + w[3:4] * back[HALO // 2 :]
        older = pltpu.roll(older, 2, 0)[HALO // 2 :]
        return (newer + older).astype(jnp.bfloat16)

    spans = (place, 2 * shards - 1 - place)

    def pair_block(s, i):
        for g in range(2):
            kvc[s * per_span + i, :, g * channels : (g + 1) * channels] = conv(
                xkv, s, i, pt, g
            )
        packed = jnp.dot(
            table[...], kvc[s * per_span + i], preferred_element_type=jnp.float32
        )
        gath[spans[s], pl.ds(pl.multiple_of(i * KEEP, KEEP), KEEP), :] = packed.astype(
            jnp.bfloat16
        )

    def query_block(s, i):
        for h in range(heads):
            qc[s * per_span + i, h] = conv(xq, s, i, qt, h)

    small[0].wait()
    small[1].wait()
    for s in range(2):
        loads["kv", s].wait()
        loop(1, per_span, functools.partial(pair_block, s))

    mate = place + 1 - 2 * lax.rem(place, 2)
    chips = shards // 2

    def peer(d):
        return lax.rem(place + 2 * d, shards)

    def span_copy(s, span, target, part, hop):
        rows = (pl.ds(0, KEEP), pl.ds(KEEP, half - KEEP))[part]
        return pltpu.make_async_remote_copy(
            src_ref=gath.at[span, rows, :],
            dst_ref=gath.at[span, rows, :],
            send_sem=span_send.at[part, s, hop],
            recv_sem=span_recv.at[part, span],
            device_id={"ctx": target},
            device_id_type=MESH,
        )

    def when(condition, act):
        @pl.when(condition)
        def _():
            act()

    def own_copies(part, act):
        for d in range(1, chips):
            target = peer(d)
            other = target + 1 - 2 * lax.rem(target, 2)
            act(span_copy(0, spans[0], target, part, d))
            when(
                target > place,
                lambda: act(span_copy(0, spans[0], other, part, shards + d)),
            )
            when(target < place, lambda: act(span_copy(1, spans[1], target, part, d)))
        act(span_copy(0, spans[0], mate, part, 0))
        when(mate < place, lambda: act(span_copy(1, spans[1], mate, part, 0)))

    def passed_copies(part, d, act):
        source = peer(d)
        upper = 2 * shards - 1 - source

        def both():
            act(span_copy(0, source, mate, part, shards + chips + d))
            act(span_copy(1, upper, mate, part, shards + chips + d))

        when(source > place, both)

    def arrive(s, q, part):
        span = (q, 2 * shards - 1 - q)[s]
        span_copy(s, span, mate, part, 0).wait_recv()

    def pass_on(part):
        for d in range(1, chips):
            source = peer(d)

            def both():
                arrive(0, source, part)
                arrive(1, source, part)

            when(source > place, both)
            passed_copies(part, d, lambda copy: copy.start())

    own_copies(1, lambda copy: copy.start())
    small[2].wait()
    small[3].wait()
    loads["q", 0].wait()
    loop(1, per_span, functools.partial(query_block, 0))
    wait_halo(0)
    for s in range(2):
        pair_block(s, 0)
    own_copies(0, lambda copy: copy.start())

    loads["q", 1].wait()
    loop(1, per_span, functools.partial(query_block, 1))
    wait_halo(1)
    for s in range(2):
        query_block(s, 0)

    block_id = functools.partial(block_of, place, shards, per_span)
    part_rows = 2 * shards * half // FAR_PARTS

    def low_copy(i):
        rows = pl.ds(pl.multiple_of(i * block, block), block)
        return pltpu.make_async_copy(out.at[rows, :], low_hbm.at[rows, :], out_sem.at[i])

    def awaited(s, q):
        passed = jnp.logical_and(lax.rem(q, 2) == lax.rem(place, 2), q > place)
        return jnp.logical_and(jnp.logical_not(passed), (q != place) if s == 0 else (q > place))

    def needed_parts(index):
        return (block_id(index) * KEEP + part_rows - 1) // part_rows

    lower_spans = needed_parts(per_span - 1) * (part_rows // half)

    def await_spans(s, low, high):
        for q in range(shards):
            wanted = jnp.logical_and(q >= low, q < high)

            @pl.when(jnp.logical_and(wanted, awaited(s, q)))
            def _():
                for part in range(2):
                    arrive(s, q, part)

    handed = [
        pltpu.make_async_copy(source, target, hand_sem.at[n])
        for n, (source, target) in enumerate(
            [
                (qc.at[pl.ds(per_span, per_span)], qc_hbm),
                (kvc.at[pl.ds(per_span, per_span)], kvc_hbm),
                (gath, gath_hbm),
            ]
        )
    ]
    handed[0].start()
    handed[1].start()

    early = lower_spans > place - lax.rem(place, 2) + 2

    @pl.when(early)
    def _():
        pass_on(1)
        pass_on(0)

    await_spans(0, 0, lower_spans)

    def step(index):
        @pl.when(jnp.logical_and(index == min(1, per_span - 1), jnp.logical_not(early)))
        def _():
            pass_on(1)
            pass_on(0)

        @pl.when(index == per_span - 1)
        def _():
            await_spans(0, lower_spans, shards)
            await_spans(1, 0, shards)
            handed[2].start()

        attend_blocks(
            qc, kvc, gath, gain, out, index, 1, block_id(index), part_rows, 1, FAR_PARTS // 2
        )
        low_copy(index).start()

    loop(0, per_span, step)
    loop(0, per_span, lambda index: low_copy(index).wait())
    for copy in handed:
        copy.wait()

    for n in range(2):

        @pl.when(jnp.logical_not(last))
        def _():
            halo_copy(n, 0, 1).wait_send()

        @pl.when(jnp.logical_not(first))
        def _():
            halo_copy(n, 1, -1).wait_send()

    for part in range(2):
        own_copies(part, lambda copy: copy.wait_send())
        for d in range(1, chips):
            passed_copies(part, d, lambda copy: copy.wait_send())


def upper_kernel(
    shards,
    per_span,
    heads,
    low_hbm,
    qc_hbm,
    kvc_hbm,
    gath_hbm,
    gain_hbm,
    out_hbm,
    qc,
    kvc,
    gath,
    gain,
    out,
    low,
    in_sem,
    q_sem,
    out_sem,
    low_sem,
):
    place = lax.axis_index("ctx")
    block = TRANSFORM_BLOCK
    span_rows = per_span * block
    part_rows = 2 * shards * per_span * KEEP // FAR_PARTS

    loads = [
        pltpu.make_async_copy(source, target, in_sem.at[n])
        for n, (source, target) in enumerate(
            [(gath_hbm, gath), (kvc_hbm, kvc), (gain_hbm, gain)]
        )
    ]

    def query_load(i):
        return pltpu.make_async_copy(qc_hbm.at[i], qc.at[i], q_sem.at[i])

    query_load(0).start()
    for copy in loads:
        copy.start()
    loop(1, per_span, lambda i: query_load(i).start())
    low_load = pltpu.make_async_copy(low_hbm, low, low_sem.at[0])
    low_store = pltpu.make_async_copy(
        low, out_hbm.at[pl.ds(0, span_rows), :], low_sem.at[1]
    )
    low_load.start()

    def out_copy(i):
        rows = pl.ds(pl.multiple_of(i * block, block), block)
        target = pl.ds(pl.multiple_of(span_rows + i * block, block), block)
        return pltpu.make_async_copy(
            out.at[rows, :], out_hbm.at[target, :], out_sem.at[i]
        )

    for copy in loads:
        copy.wait()

    count = 2 - per_span % 2

    def step(n):
        i = n * count
        for k in range(count):
            query_load(i + k).wait()
        block_id = block_of(place, shards, per_span, per_span + i)
        least = FAR_PARTS // 2
        attend_blocks(
            qc, kvc, gath, gain, out, i, count, block_id, part_rows, least, FAR_PARTS
        )
        for k in range(count):
            out_copy(i + k).start()

        @pl.when(n == 0)
        def _():
            low_load.wait()
            low_store.start()

    loop(0, per_span // count, step)
    loop(0, per_span, lambda i: out_copy(i).wait())
    low_store.wait()


def attention(queries, pairs, query_taps, pair_taps, out_gain, shards):
    rows, columns = queries.shape
    span_rows = rows // 2
    per_span = span_rows // TRANSFORM_BLOCK
    heads = columns // HEAD_CHANNELS
    half = per_span * KEEP
    blocks = 2 * per_span
    bf16, f32 = jnp.bfloat16, jnp.float32
    width = 2 * HEAD_CHANNELS
    hbm = pl.BlockSpec(memory_space=pltpu.HBM)
    dma = pltpu.SemaphoreType.DMA
    gain = out_gain.reshape(1, columns)
    half_q = (per_span, heads, TRANSFORM_BLOCK, HEAD_CHANNELS)
    half_kv = (per_span, TRANSFORM_BLOCK, width)
    all_packed = (2 * shards, half, width)
    handed = pl.pallas_call(
        functools.partial(kernel, shards, per_span, heads),
        out_shape=[
            jax.ShapeDtypeStruct((span_rows, columns), bf16),
            jax.ShapeDtypeStruct(half_q, bf16),
            jax.ShapeDtypeStruct(half_kv, bf16),
            jax.ShapeDtypeStruct(all_packed, bf16),
        ],
        in_specs=[hbm] * 6,
        out_specs=[hbm] * 4,
        scratch_shapes=[
            pltpu.VMEM((2, HALO + span_rows, columns), bf16),
            pltpu.VMEM((2, HALO + span_rows, width), bf16),
            pltpu.VMEM((TAPS, columns), f32),
            pltpu.VMEM((TAPS, width), f32),
            pltpu.VMEM((1, columns), f32),
            pltpu.VMEM((KEEP, TRANSFORM_BLOCK), bf16),
            pltpu.VMEM((blocks, heads, TRANSFORM_BLOCK, HEAD_CHANNELS), bf16),
            pltpu.VMEM((blocks, TRANSFORM_BLOCK, width), bf16),
            pltpu.VMEM(all_packed, bf16),
            pltpu.VMEM((span_rows, columns), bf16),
            dma((4,)),
            dma((4,)),
            dma((2,)),
            dma((2, 2)),
            dma((2, 2)),
            dma((2, 2, 2 * shards)),
            dma((2, 2 * shards)),
            dma((per_span,)),
            dma((3,)),
        ],
        compiler_params=pltpu.CompilerParams(
            collective_id=0, has_side_effects=True, vmem_limit_bytes=62 * 1024 * 1024
        ),
        name="exchange_and_lower",
    )(
        queries,
        pairs,
        query_taps,
        pair_taps,
        gain,
        jnp.asarray(dct_table()),
    )
    return pl.pallas_call(
        functools.partial(upper_kernel, shards, per_span, heads),
        out_shape=jax.ShapeDtypeStruct((rows, columns), bf16),
        in_specs=[hbm] * 5,
        out_specs=hbm,
        scratch_shapes=[
            pltpu.VMEM(half_q, bf16),
            pltpu.VMEM(half_kv, bf16),
            pltpu.VMEM(all_packed, bf16),
            pltpu.VMEM((1, columns), f32),
            pltpu.VMEM((span_rows, columns), bf16),
            pltpu.VMEM((span_rows, columns), bf16),
            dma((3,)),
            dma((per_span,)),
            dma((per_span,)),
            dma((2,)),
        ],
        compiler_params=pltpu.CompilerParams(vmem_limit_bytes=62 * 1024 * 1024),
        name="upper",
    )(*handed, gain)


def from_partner(block, axis, apart):
    count = lax.axis_size(axis)
    route = []
    for low in range(count):
        high = low | 1 << apart
        if high != low and high < count:
            route += [(low, high), (high, low)]
    return lax.ppermute(block, axis, route)


def per_device(queries, keys_values, query_taps, pair_taps, out_gain):
    member = lax.axis_index("mp")
    width = keys_values.shape[1]
    rounds = (2 * HEAD_CHANNELS // width).bit_length() - 1

    def join(mine, bit):
        other = from_partner(mine, "mp", bit)
        lower = member // 2**bit % 2 == 0
        return jnp.where(
            lower, jnp.concatenate([mine, other], 1), jnp.concatenate([other, mine], 1)
        )

    for bit in range(rounds):
        keys_values = join(keys_values, bit)
        pair_taps = join(pair_taps, bit)
    return attention(
        queries, keys_values, query_taps, pair_taps, out_gain, lax.axis_size("ctx")
    )


def solution(mesh):
    in_specs = (P("ctx", "mp"), P("ctx", "mp"), P(None, "mp"), P(None, "mp"), P("mp"))
    out_specs = P("ctx", "mp")
    return jax.shard_map(
        per_device, mesh=mesh, in_specs=in_specs, out_specs=out_specs, check_vma=False
    )
```

```python
import functools
import math

import jax
import jax.numpy as jnp
import numpy as np
from jax import lax
from jax.experimental import pallas as pl
from jax.experimental.pallas import tpu as pltpu
from jax.sharding import PartitionSpec as P

HEAD_CHANNELS = 128
TAPS = 4
TRANSFORM_BLOCK = 128
KEEP = 16
HALO = 16
FAR_PARTS = 4

NEGATIVE = -1e30
EPSILON = 1e-06
MESH = pl.DeviceIdType.MESH


def dct_table():
    frequency = np.arange(KEEP, dtype=np.float32)[:, None]
    offset = np.arange(TRANSFORM_BLOCK, dtype=np.float32)[None, :]
    angle = np.float32(math.pi) * (offset + np.float32(0.5)) * frequency
    table = np.cos(angle / np.float32(TRANSFORM_BLOCK)) * np.float32(
        math.sqrt(2.0 / TRANSFORM_BLOCK)
    )
    table = np.where(frequency == 0.0, table * np.float32(math.sqrt(0.5)), table)
    return table.astype(jnp.bfloat16)


def loop(low, high, body):
    def step(i, carry):
        body(i)
        return carry

    lax.fori_loop(low, high, step, 0)


def block_of(place, shards, per_span, index):
    upper = index // per_span
    span = place + upper * (2 * shards - 1 - 2 * place)
    return span * per_span + lax.rem(index, per_span)


def attend_blocks(qc, kvc, gath, turned, gain, out, index, count, block_id, part_rows, least, most):
    needed = ((block_id + count - 1) * KEEP + part_rows - 1) // part_rows
    for parts in range(least, most + 1):
        fits = needed <= least if parts == least else needed == parts

        @pl.when(fits)
        def _():
            attend(
                qc, kvc, gath, turned, gain, out, index, count, block_id, part_rows, parts
            )


def attend(qc, kvc, gath, turned, gain, out, index, count, block_id, part_rows, parts):
    block, channels = TRANSFORM_BLOCK, HEAD_CHANNELS
    heads, half = qc.shape[1], gath.shape[1]
    scale = math.log2(math.e) / math.sqrt(channels)
    row_id = lax.broadcasted_iota(jnp.int32, (block, block), 0)
    column_id = lax.broadcasted_iota(jnp.int32, (block, block), 1)
    near_bias = jnp.where(row_id >= column_id, 0.0, NEGATIVE)
    far_rows = parts * part_rows
    open_rows = block + far_rows - part_rows
    far = gath[: far_rows // half].reshape(far_rows, 2 * channels)
    far_ids = lax.broadcasted_iota(jnp.int32, (1, part_rows), 1) + (far_rows - part_rows)
    far_keys = far[:, :channels].T if turned is None else turned[:, :far_rows]
    some = min(heads, 2)
    for step in range(count):
        near = kvc[index + step]
        far_bias = jnp.where(far_ids < (block_id + step) * KEEP, 0.0, NEGATIVE)
        keys = jnp.concatenate([near[:, :channels].T, far_keys], 1)
        values = jnp.concatenate([near[:, channels:], far[:, channels:]], 0)
        values = jnp.concatenate([values, jnp.ones_like(values)], 1)
        rows = pl.ds(pl.multiple_of((index + step) * block, block), block)
        for begin in range(0, heads, some):
            query = qc[index + step, begin : begin + some].reshape(some * block, channels)
            scores = jnp.dot(query, keys, preferred_element_type=jnp.float32)
            near_scores = (
                scores[:, :block].reshape(some, block, block) + near_bias[None]
            ).reshape(some * block, block)
            pieces = [near_scores, scores[:, open_rows:] + far_bias]
            if parts > 1:
                pieces.insert(1, scores[:, block:open_rows])
            scores = jnp.concatenate(pieces, 1)
            top = jnp.max(scores, -1, keepdims=True)
            weights = jnp.exp2((scores - top) * scale).astype(jnp.bfloat16)
            both = jnp.dot(weights, values, preferred_element_type=jnp.float32)
            summed, total = both[:, :channels], both[:, channels:]
            mean = jnp.mean(summed * summed, -1, keepdims=True)
            normed = summed * lax.rsqrt(mean + EPSILON * (total * total))
            for h in range(some):
                columns = pl.ds((begin + h) * channels, channels)
                out[rows, columns] = (
                    normed[h * block : (h + 1) * block] * gain[:, columns]
                ).astype(jnp.bfloat16)


def kernel(
    shards,
    per_span,
    heads,
    q_hbm,
    kv_hbm,
    qt_hbm,
    pt_hbm,
    gahbm,
    table_hbm,
    low_hbm,
    qc_hbm,
    kvc_hbm,
    gath_hbm,
    xq,
    xkv,
    qt,
    pt,
    gain,
    table,
    qc,
    kvc,
    gath,
    out,
    in_sem,
    small_sem,
    own_halo_sem,
    halo_send,
    halo_recv,
    span_send,
    span_recv,
    out_sem,
    hand_sem,
):
    place = lax.axis_index("ctx")
    block = TRANSFORM_BLOCK
    span_rows = per_span * block
    half = per_span * KEEP
    channels = HEAD_CHANNELS

    loads = {}
    for s in range(2):
        loads["kv", s] = pltpu.make_async_copy(
            kv_hbm.at[pl.ds(s * span_rows, span_rows), :],
            xkv.at[s, pl.ds(HALO, span_rows), :],
            in_sem.at[s],
        )
        loads["q", s] = pltpu.make_async_copy(
            q_hbm.at[pl.ds(s * span_rows, span_rows), :],
            xq.at[s, pl.ds(HALO, span_rows), :],
            in_sem.at[2 + s],
        )
    small = [
        pltpu.make_async_copy(source, target, small_sem.at[n])
        for n, (source, target) in enumerate(
            [(pt_hbm, pt), (table_hbm, table), (qt_hbm, qt), (gahbm, gain)]
        )
    ]
    loads["kv", 0].start()
    loads["kv", 1].start()
    for copy in small:
        copy.start()
    loads["q", 0].start()
    loads["q", 1].start()

    barrier = pltpu.get_barrier_semaphore()
    for d in range(1, shards):
        pl.semaphore_signal(
            barrier,
            inc=1,
            device_id={"ctx": lax.rem(place + d, shards)},
            device_id_type=MESH,
        )
    pl.semaphore_wait(barrier, shards - 1)

    def halo_copy(n, s, step):
        source, target = ((kv_hbm, xkv), (q_hbm, xq))[n]
        return pltpu.make_async_remote_copy(
            src_ref=source.at[pl.ds((s + 1) * span_rows - HALO, HALO), :],
            dst_ref=target.at[s, pl.ds(0, HALO), :],
            send_sem=halo_send.at[n, s],
            recv_sem=halo_recv.at[n, s],
            device_id={"ctx": lax.rem(place + step + shards, shards)},
            device_id_type=MESH,
        )

    def own_halo(n):
        source, target = ((kv_hbm, xkv), (q_hbm, xq))[n]
        return pltpu.make_async_copy(
            source.at[pl.ds(span_rows - HALO, HALO), :],
            target.at[1, pl.ds(0, HALO), :],
            own_halo_sem.at[n],
        )

    first = place == 0
    last = place == shards - 1
    for n in range(2):

        @pl.when(jnp.logical_not(last))
        def _():
            halo_copy(n, 0, 1).start()

        @pl.when(jnp.logical_not(first))
        def _():
            halo_copy(n, 1, -1).start()

        @pl.when(last)
        def _():
            own_halo(n).start()

    @pl.when(first)
    def _():
        xkv[0, :HALO, :] = jnp.zeros((HALO, xkv.shape[2]), xkv.dtype)
        xq[0, :HALO, :] = jnp.zeros((HALO, xq.shape[2]), xq.dtype)

    for q in range(shards - 1):

        @pl.when(q < place)
        def _():
            gath[2 * shards - 1 - q] = jnp.zeros(gath.shape[1:], gath.dtype)

    def wait_halo(n):
        @pl.when(jnp.logical_not(first))
        def _():
            halo_copy(n, 0, 1).wait_recv()

        @pl.when(jnp.logical_not(last))
        def _():
            halo_copy(n, 1, -1).wait_recv()

        @pl.when(last)
        def _():
            own_halo(n).wait()

    def conv(source, s, i, taps, g):
        columns = pl.ds(g * channels, channels)
        rows = pl.ds(pl.multiple_of(i * block, block), block + HALO)
        x = source[s, rows, columns].astype(jnp.float32)
        w = taps[:, columns]
        back = pltpu.roll(x, 1, 0)
        newer = w[0:1] * x[HALO:] + w[1:2] * back[HALO:]
        older = w[2:3] * x[HALO // 2 :] + w[3:4] * back[HALO // 2 :]
        older = pltpu.roll(older, 2, 0)[HALO // 2 :]
        return (newer + older).astype(jnp.bfloat16)

    spans = (place, 2 * shards - 1 - place)

    def pair_block(s, i):
        for g in range(2):
            kvc[s * per_span + i, :, g * channels : (g + 1) * channels] = conv(
                xkv, s, i, pt, g
            )
        packed = jnp.dot(
            table[...], kvc[s * per_span + i], preferred_element_type=jnp.float32
        )
        gath[spans[s], pl.ds(pl.multiple_of(i * KEEP, KEEP), KEEP), :] = packed.astype(
            jnp.bfloat16
        )

    def query_block(s, i):
        for h in range(heads):
            qc[s * per_span + i, h] = conv(xq, s, i, qt, h)

    small[0].wait()
    small[1].wait()
    for s in range(2):
        loads["kv", s].wait()
        loop(1, per_span, functools.partial(pair_block, s))

    mate = place + 1 - 2 * lax.rem(place, 2)
    chips = shards // 2

    def peer(d):
        return lax.rem(place + 2 * d, shards)

    def span_copy(s, span, target, part, hop):
        rows = (pl.ds(0, KEEP), pl.ds(KEEP, half - KEEP))[part]
        return pltpu.make_async_remote_copy(
            src_ref=gath.at[span, rows, :],
            dst_ref=gath.at[span, rows, :],
            send_sem=span_send.at[part, s, hop],
            recv_sem=span_recv.at[part, span],
            device_id={"ctx": target},
            device_id_type=MESH,
        )

    def when(condition, act):
        @pl.when(condition)
        def _():
            act()

    def own_copies(part, act):
        for d in range(1, chips):
            target = peer(d)
            other = target + 1 - 2 * lax.rem(target, 2)
            act(span_copy(0, spans[0], target, part, d))
            when(
                target > place,
                lambda: act(span_copy(0, spans[0], other, part, shards + d)),
            )
            when(target < place, lambda: act(span_copy(1, spans[1], target, part, d)))
        act(span_copy(0, spans[0], mate, part, 0))
        when(mate < place, lambda: act(span_copy(1, spans[1], mate, part, 0)))

    def passed_copies(part, d, act):
        source = peer(d)
        upper = 2 * shards - 1 - source

        def both():
            act(span_copy(0, source, mate, part, shards + chips + d))
            act(span_copy(1, upper, mate, part, shards + chips + d))

        when(source > place, both)

    def arrive(s, q, part):
        span = (q, 2 * shards - 1 - q)[s]
        span_copy(s, span, mate, part, 0).wait_recv()

    def pass_on(part):
        for d in range(1, chips):
            source = peer(d)

            def both():
                arrive(0, source, part)
                arrive(1, source, part)

            when(source > place, both)
            passed_copies(part, d, lambda copy: copy.start())

    own_copies(1, lambda copy: copy.start())
    small[2].wait()
    small[3].wait()
    loads["q", 0].wait()
    loop(1, per_span, functools.partial(query_block, 0))
    wait_halo(0)
    for s in range(2):
        pair_block(s, 0)
    own_copies(0, lambda copy: copy.start())

    loads["q", 1].wait()
    loop(1, per_span, functools.partial(query_block, 1))
    pass_on(1)
    wait_halo(1)
    for s in range(2):
        query_block(s, 0)

    block_id = functools.partial(block_of, place, shards, per_span)
    part_rows = 2 * shards * half // FAR_PARTS

    def low_copy(i):
        rows = pl.ds(pl.multiple_of(i * block, block), block)
        return pltpu.make_async_copy(out.at[rows, :], low_hbm.at[rows, :], out_sem.at[i])

    def awaited(s, q):
        passed = jnp.logical_and(lax.rem(q, 2) == lax.rem(place, 2), q > place)
        return jnp.logical_and(jnp.logical_not(passed), (q != place) if s == 0 else (q > place))

    def needed_parts(index):
        return (block_id(index) * KEEP + part_rows - 1) // part_rows

    lower_spans = needed_parts(per_span - 1) * (part_rows // half)

    def await_spans(s, low, high):
        for q in range(shards):
            wanted = jnp.logical_and(q >= low, q < high)

            @pl.when(jnp.logical_and(wanted, awaited(s, q)))
            def _():
                for part in range(2):
                    arrive(s, q, part)

    handed = [
        pltpu.make_async_copy(source, target, hand_sem.at[n])
        for n, (source, target) in enumerate(
            [
                (qc.at[pl.ds(per_span, per_span)], qc_hbm),
                (kvc.at[pl.ds(per_span, per_span)], kvc_hbm),
                (gath, gath_hbm),
            ]
        )
    ]
    handed[0].start()
    handed[1].start()

    pass_on(0)
    await_spans(0, 0, lower_spans)

    count = 2 - per_span % 2

    def step(n):
        index = n * count

        @pl.when(n == per_span // count - 1)
        def _():
            await_spans(0, lower_spans, shards)
            await_spans(1, 0, shards)
            handed[2].start()

        most = FAR_PARTS // 2
        attend_blocks(
            qc, kvc, gath, None, gain, out, index, count, block_id(index), part_rows, 1, most
        )
        for k in range(count):
            low_copy(index + k).start()

    loop(0, per_span // count, step)
    loop(0, per_span, lambda index: low_copy(index).wait())
    for copy in handed:
        copy.wait()

    for n in range(2):

        @pl.when(jnp.logical_not(last))
        def _():
            halo_copy(n, 0, 1).wait_send()

        @pl.when(jnp.logical_not(first))
        def _():
            halo_copy(n, 1, -1).wait_send()

    for part in range(2):
        own_copies(part, lambda copy: copy.wait_send())
        for d in range(1, chips):
            passed_copies(part, d, lambda copy: copy.wait_send())


def upper_kernel(
    shards,
    per_span,
    heads,
    low_hbm,
    qc_hbm,
    kvc_hbm,
    gath_hbm,
    gain_hbm,
    out_hbm,
    qc,
    kvc,
    gath,
    gain,
    out,
    low,
    turned,
    in_sem,
    q_sem,
    out_sem,
    low_sem,
):
    place = lax.axis_index("ctx")
    block = TRANSFORM_BLOCK
    span_rows = per_span * block
    part_rows = 2 * shards * per_span * KEEP // FAR_PARTS

    loads = [
        pltpu.make_async_copy(source, target, in_sem.at[n])
        for n, (source, target) in enumerate(
            [(gath_hbm, gath), (kvc_hbm, kvc), (gain_hbm, gain)]
        )
    ]

    def query_load(i):
        return pltpu.make_async_copy(qc_hbm.at[i], qc.at[i], q_sem.at[i])

    query_load(0).start()
    for copy in loads:
        copy.start()
    loop(1, per_span, lambda i: query_load(i).start())
    low_load = pltpu.make_async_copy(low_hbm, low, low_sem.at[0])
    low_store = pltpu.make_async_copy(
        low, out_hbm.at[pl.ds(0, span_rows), :], low_sem.at[1]
    )
    low_load.start()

    def out_copy(i):
        rows = pl.ds(pl.multiple_of(i * block, block), block)
        target = pl.ds(pl.multiple_of(span_rows + i * block, block), block)
        return pltpu.make_async_copy(
            out.at[rows, :], out_hbm.at[target, :], out_sem.at[i]
        )

    for copy in loads:
        copy.wait()
    turned[...] = gath[...].reshape(turned.shape[1], -1)[:, :HEAD_CHANNELS].T

    count = 2 - per_span % 2

    def step(n):
        i = n * count
        for k in range(count):
            query_load(i + k).wait()
        block_id = block_of(place, shards, per_span, per_span + i)
        least = FAR_PARTS // 2
        attend_blocks(
            qc, kvc, gath, turned, gain, out, i, count, block_id, part_rows, least, FAR_PARTS
        )
        for k in range(count):
            out_copy(i + k).start()

        @pl.when(n == 0)
        def _():
            low_load.wait()
            low_store.start()

    loop(0, per_span // count, step)
    loop(0, per_span, lambda i: out_copy(i).wait())
    low_store.wait()


def attention(queries, pairs, query_taps, pair_taps, out_gain, shards):
    rows, columns = queries.shape
    span_rows = rows // 2
    per_span = span_rows // TRANSFORM_BLOCK
    heads = columns // HEAD_CHANNELS
    half = per_span * KEEP
    blocks = 2 * per_span
    bf16, f32 = jnp.bfloat16, jnp.float32
    width = 2 * HEAD_CHANNELS
    hbm = pl.BlockSpec(memory_space=pltpu.HBM)
    dma = pltpu.SemaphoreType.DMA
    gain = out_gain.reshape(1, columns)
    half_q = (per_span, heads, TRANSFORM_BLOCK, HEAD_CHANNELS)
    half_kv = (per_span, TRANSFORM_BLOCK, width)
    all_packed = (2 * shards, half, width)
    handed = pl.pallas_call(
        functools.partial(kernel, shards, per_span, heads),
        out_shape=[
            jax.ShapeDtypeStruct((span_rows, columns), bf16),
            jax.ShapeDtypeStruct(half_q, bf16),
            jax.ShapeDtypeStruct(half_kv, bf16),
            jax.ShapeDtypeStruct(all_packed, bf16),
        ],
        in_specs=[hbm] * 6,
        out_specs=[hbm] * 4,
        scratch_shapes=[
            pltpu.VMEM((2, HALO + span_rows, columns), bf16),
            pltpu.VMEM((2, HALO + span_rows, width), bf16),
            pltpu.VMEM((TAPS, columns), f32),
            pltpu.VMEM((TAPS, width), f32),
            pltpu.VMEM((1, columns), f32),
            pltpu.VMEM((KEEP, TRANSFORM_BLOCK), bf16),
            pltpu.VMEM((blocks, heads, TRANSFORM_BLOCK, HEAD_CHANNELS), bf16),
            pltpu.VMEM((blocks, TRANSFORM_BLOCK, width), bf16),
            pltpu.VMEM(all_packed, bf16),
            pltpu.VMEM((span_rows, columns), bf16),
            dma((4,)),
            dma((4,)),
            dma((2,)),
            dma((2, 2)),
            dma((2, 2)),
            dma((2, 2, 2 * shards)),
            dma((2, 2 * shards)),
            dma((per_span,)),
            dma((3,)),
        ],
        compiler_params=pltpu.CompilerParams(
            collective_id=0, has_side_effects=True, vmem_limit_bytes=62 * 1024 * 1024
        ),
        name="exchange_and_lower",
    )(
        queries,
        pairs,
        query_taps,
        pair_taps,
        gain,
        jnp.asarray(dct_table()),
    )
    return pl.pallas_call(
        functools.partial(upper_kernel, shards, per_span, heads),
        out_shape=jax.ShapeDtypeStruct((rows, columns), bf16),
        in_specs=[hbm] * 5,
        out_specs=hbm,
        scratch_shapes=[
            pltpu.VMEM(half_q, bf16),
            pltpu.VMEM(half_kv, bf16),
            pltpu.VMEM(all_packed, bf16),
            pltpu.VMEM((1, columns), f32),
            pltpu.VMEM((span_rows, columns), bf16),
            pltpu.VMEM((span_rows, columns), bf16),
            pltpu.VMEM((HEAD_CHANNELS, 2 * shards * half), bf16),
            dma((3,)),
            dma((per_span,)),
            dma((per_span,)),
            dma((2,)),
        ],
        compiler_params=pltpu.CompilerParams(vmem_limit_bytes=62 * 1024 * 1024),
        name="upper",
    )(*handed, gain)


def from_partner(block, axis, apart):
    count = lax.axis_size(axis)
    route = []
    for low in range(count):
        high = low | 1 << apart
        if high != low and high < count:
            route += [(low, high), (high, low)]
    return lax.ppermute(block, axis, route)


def per_device(queries, keys_values, query_taps, pair_taps, out_gain):
    member = lax.axis_index("mp")
    width = keys_values.shape[1]
    rounds = (2 * HEAD_CHANNELS // width).bit_length() - 1

    def join(mine, bit):
        other = from_partner(mine, "mp", bit)
        lower = member // 2**bit % 2 == 0
        return jnp.where(
            lower, jnp.concatenate([mine, other], 1), jnp.concatenate([other, mine], 1)
        )

    for bit in range(rounds):
        keys_values = join(keys_values, bit)
        pair_taps = join(pair_taps, bit)
    return attention(
        queries, keys_values, query_taps, pair_taps, out_gain, lax.axis_size("ctx")
    )


def solution(mesh):
    in_specs = (P("ctx", "mp"), P("ctx", "mp"), P(None, "mp"), P(None, "mp"), P("mp"))
    out_specs = P("ctx", "mp")
    return jax.shard_map(
        per_device, mesh=mesh, in_specs=in_specs, out_specs=out_specs, check_vma=False
    )
```

```python
import functools
import math

import jax
import jax.numpy as jnp
import numpy as np
from jax import lax
from jax.experimental import pallas as pl
from jax.experimental.pallas import tpu as pltpu
from jax.sharding import PartitionSpec as P

HEAD_CHANNELS = 128
TAPS = 4
TRANSFORM_BLOCK = 128
KEEP = 16
HALO = 16
FAR_PARTS = 4

NEGATIVE = -1e30
EPSILON = 1e-06
MESH = pl.DeviceIdType.MESH


def dct_table():
    frequency = np.arange(KEEP, dtype=np.float32)[:, None]
    offset = np.arange(TRANSFORM_BLOCK, dtype=np.float32)[None, :]
    angle = np.float32(math.pi) * (offset + np.float32(0.5)) * frequency
    table = np.cos(angle / np.float32(TRANSFORM_BLOCK)) * np.float32(
        math.sqrt(2.0 / TRANSFORM_BLOCK)
    )
    table = np.where(frequency == 0.0, table * np.float32(math.sqrt(0.5)), table)
    return table.astype(jnp.bfloat16)


def nt_dot(left, right):
    return lax.dot_general(
        left, right, (((1,), (1,)), ((), ())), preferred_element_type=jnp.float32
    )


def loop(low, high, body):
    def step(i, carry):
        body(i)
        return carry

    lax.fori_loop(low, high, step, 0)


def block_of(place, shards, per_span, index):
    upper = index // per_span
    span = place + upper * (2 * shards - 1 - 2 * place)
    return span * per_span + lax.rem(index, per_span)


def attend_blocks(qc, kvc, gath, gain, out, index, count, block_id, part_rows, least, most):
    needed = ((block_id + count - 1) * KEEP + part_rows - 1) // part_rows
    for parts in range(least, most + 1):
        fits = needed <= least if parts == least else needed == parts

        @pl.when(fits)
        def _():
            attend(
                qc, kvc, gath, gain, out, index, count, block_id, part_rows, parts
            )


def attend(qc, kvc, gath, gain, out, index, count, block_id, part_rows, parts):
    block, channels = TRANSFORM_BLOCK, HEAD_CHANNELS
    heads, half = qc.shape[1], gath.shape[1]
    scale = math.log2(math.e) / math.sqrt(channels)
    row_id = lax.broadcasted_iota(jnp.int32, (block, block), 0)
    column_id = lax.broadcasted_iota(jnp.int32, (block, block), 1)
    near_bias = jnp.where(row_id >= column_id, 0.0, NEGATIVE)
    far_rows = parts * part_rows
    open_rows = block + far_rows - part_rows
    far = gath[: far_rows // half].reshape(far_rows, 2 * channels)
    far_ids = lax.broadcasted_iota(jnp.int32, (1, part_rows), 1) + (far_rows - part_rows)
    some = min(heads, 2)
    for step in range(count):
        near = kvc[index + step]
        far_bias = jnp.where(far_ids < (block_id + step) * KEEP, 0.0, NEGATIVE)
        keys = jnp.concatenate([near[:, :channels], far[:, :channels]], 0)
        values = jnp.concatenate([near[:, channels:], far[:, channels:]], 0)
        values = jnp.concatenate([values, jnp.ones_like(values)], 1)
        rows = pl.ds(pl.multiple_of((index + step) * block, block), block)
        for begin in range(0, heads, some):
            query = qc[index + step, begin : begin + some].reshape(some * block, channels)
            scores = nt_dot(query, keys)
            near_scores = (
                scores[:, :block].reshape(some, block, block) + near_bias[None]
            ).reshape(some * block, block)
            pieces = [near_scores, scores[:, open_rows:] + far_bias]
            if parts > 1:
                pieces.insert(1, scores[:, block:open_rows])
            scores = jnp.concatenate(pieces, 1)
            top = jnp.max(scores, -1, keepdims=True)
            weights = jnp.exp2((scores - top) * scale).astype(jnp.bfloat16)
            both = jnp.dot(weights, values, preferred_element_type=jnp.float32)
            summed, total = both[:, :channels], both[:, channels:]
            mean = jnp.mean(summed * summed, -1, keepdims=True)
            normed = summed * lax.rsqrt(mean + EPSILON * (total * total))
            for h in range(some):
                columns = pl.ds((begin + h) * channels, channels)
                out[rows, columns] = (
                    normed[h * block : (h + 1) * block] * gain[:, columns]
                ).astype(jnp.bfloat16)


def kernel(
    shards,
    per_span,
    heads,
    q_hbm,
    kv_hbm,
    qt_hbm,
    pt_hbm,
    gahbm,
    table_hbm,
    low_hbm,
    qc_hbm,
    kvc_hbm,
    gath_hbm,
    xq,
    xkv,
    qt,
    pt,
    gain,
    table,
    qc,
    kvc,
    gath,
    out,
    in_sem,
    small_sem,
    own_halo_sem,
    halo_send,
    halo_recv,
    span_send,
    span_recv,
    out_sem,
    hand_sem,
):
    place = lax.axis_index("ctx")
    block = TRANSFORM_BLOCK
    span_rows = per_span * block
    half = per_span * KEEP
    channels = HEAD_CHANNELS

    loads = {}
    for s in range(2):
        loads["kv", s] = pltpu.make_async_copy(
            kv_hbm.at[pl.ds(s * span_rows, span_rows), :],
            xkv.at[s, pl.ds(HALO, span_rows), :],
            in_sem.at[s],
        )
        loads["q", s] = pltpu.make_async_copy(
            q_hbm.at[pl.ds(s * span_rows, span_rows), :],
            xq.at[s, pl.ds(HALO, span_rows), :],
            in_sem.at[2 + s],
        )
    small = [
        pltpu.make_async_copy(source, target, small_sem.at[n])
        for n, (source, target) in enumerate(
            [(pt_hbm, pt), (table_hbm, table), (qt_hbm, qt), (gahbm, gain)]
        )
    ]
    loads["kv", 0].start()
    loads["kv", 1].start()
    for copy in small:
        copy.start()
    loads["q", 0].start()
    loads["q", 1].start()

    barrier = pltpu.get_barrier_semaphore()
    for d in range(1, shards):
        pl.semaphore_signal(
            barrier,
            inc=1,
            device_id={"ctx": lax.rem(place + d, shards)},
            device_id_type=MESH,
        )
    pl.semaphore_wait(barrier, shards - 1)

    def halo_copy(n, s, step):
        source, target = ((kv_hbm, xkv), (q_hbm, xq))[n]
        return pltpu.make_async_remote_copy(
            src_ref=source.at[pl.ds((s + 1) * span_rows - HALO, HALO), :],
            dst_ref=target.at[s, pl.ds(0, HALO), :],
            send_sem=halo_send.at[n, s],
            recv_sem=halo_recv.at[n, s],
            device_id={"ctx": lax.rem(place + step + shards, shards)},
            device_id_type=MESH,
        )

    def own_halo(n):
        source, target = ((kv_hbm, xkv), (q_hbm, xq))[n]
        return pltpu.make_async_copy(
            source.at[pl.ds(span_rows - HALO, HALO), :],
            target.at[1, pl.ds(0, HALO), :],
            own_halo_sem.at[n],
        )

    first = place == 0
    last = place == shards - 1
    for n in range(2):

        @pl.when(jnp.logical_not(last))
        def _():
            halo_copy(n, 0, 1).start()

        @pl.when(jnp.logical_not(first))
        def _():
            halo_copy(n, 1, -1).start()

        @pl.when(last)
        def _():
            own_halo(n).start()

    @pl.when(first)
    def _():
        xkv[0, :HALO, :] = jnp.zeros((HALO, xkv.shape[2]), xkv.dtype)
        xq[0, :HALO, :] = jnp.zeros((HALO, xq.shape[2]), xq.dtype)

    for q in range(shards - 1):

        @pl.when(q < place)
        def _():
            gath[2 * shards - 1 - q] = jnp.zeros(gath.shape[1:], gath.dtype)

    def wait_halo(n):
        @pl.when(jnp.logical_not(first))
        def _():
            halo_copy(n, 0, 1).wait_recv()

        @pl.when(jnp.logical_not(last))
        def _():
            halo_copy(n, 1, -1).wait_recv()

        @pl.when(last)
        def _():
            own_halo(n).wait()

    def conv(source, s, i, taps, g):
        columns = pl.ds(g * channels, channels)
        rows = pl.ds(pl.multiple_of(i * block, block), block + HALO)
        x = source[s, rows, columns].astype(jnp.float32)
        w = taps[:, columns]
        back = pltpu.roll(x, 1, 0)
        newer = w[0:1] * x[HALO:] + w[1:2] * back[HALO:]
        older = w[2:3] * x[HALO // 2 :] + w[3:4] * back[HALO // 2 :]
        older = pltpu.roll(older, 2, 0)[HALO // 2 :]
        return (newer + older).astype(jnp.bfloat16)

    spans = (place, 2 * shards - 1 - place)

    def pair_block(s, i):
        for g in range(2):
            kvc[s * per_span + i, :, g * channels : (g + 1) * channels] = conv(
                xkv, s, i, pt, g
            )
        packed = jnp.dot(
            table[...], kvc[s * per_span + i], preferred_element_type=jnp.float32
        )
        gath[spans[s], pl.ds(pl.multiple_of(i * KEEP, KEEP), KEEP), :] = packed.astype(
            jnp.bfloat16
        )

    def query_block(s, i):
        for h in range(heads):
            qc[s * per_span + i, h] = conv(xq, s, i, qt, h)

    small[0].wait()
    small[1].wait()
    for s in range(2):
        loads["kv", s].wait()
        loop(1, per_span, functools.partial(pair_block, s))

    mate = place + 1 - 2 * lax.rem(place, 2)
    chips = shards // 2

    def peer(d):
        return lax.rem(place + 2 * d, shards)

    def span_copy(s, span, target, part, hop):
        rows = (pl.ds(0, KEEP), pl.ds(KEEP, half - KEEP))[part]
        return pltpu.make_async_remote_copy(
            src_ref=gath.at[span, rows, :],
            dst_ref=gath.at[span, rows, :],
            send_sem=span_send.at[part, s, hop],
            recv_sem=span_recv.at[part, span],
            device_id={"ctx": target},
            device_id_type=MESH,
        )

    def when(condition, act):
        @pl.when(condition)
        def _():
            act()

    def own_copies(part, act):
        for d in range(1, chips):
            target = peer(d)
            other = target + 1 - 2 * lax.rem(target, 2)
            act(span_copy(0, spans[0], target, part, d))
            when(
                jnp.logical_or(target > place, part == 0),
                lambda: act(span_copy(0, spans[0], other, part, shards + d)),
            )
            when(target < place, lambda: act(span_copy(1, spans[1], target, part, d)))
            if part == 0:
                when(
                    target < place,
                    lambda: act(span_copy(1, spans[1], other, part, shards + d)),
                )
        act(span_copy(0, spans[0], mate, part, 0))
        when(mate < place, lambda: act(span_copy(1, spans[1], mate, part, 0)))

    def passed_copies(part, d, act):
        source = peer(d)
        upper = 2 * shards - 1 - source

        def both():
            act(span_copy(0, source, mate, part, shards + chips + d))
            act(span_copy(1, upper, mate, part, shards + chips + d))

        when(source > place, both)

    def arrive(s, q, part):
        span = (q, 2 * shards - 1 - q)[s]
        span_copy(s, span, mate, part, 0).wait_recv()

    def pass_on(part):
        for d in range(1, chips):
            source = peer(d)

            def both():
                arrive(0, source, part)
                arrive(1, source, part)

            when(source > place, both)
            passed_copies(part, d, lambda copy: copy.start())

    own_copies(1, lambda copy: copy.start())
    small[2].wait()
    small[3].wait()
    loads["q", 0].wait()
    loop(1, per_span, functools.partial(query_block, 0))
    wait_halo(0)
    for s in range(2):
        pair_block(s, 0)
    own_copies(0, lambda copy: copy.start())

    loads["q", 1].wait()
    loop(1, per_span, functools.partial(query_block, 1))
    wait_halo(1)
    for s in range(2):
        query_block(s, 0)

    block_id = functools.partial(block_of, place, shards, per_span)
    part_rows = 2 * shards * half // FAR_PARTS

    def low_copy(i):
        rows = pl.ds(pl.multiple_of(i * block, block), block)
        return pltpu.make_async_copy(out.at[rows, :], low_hbm.at[rows, :], out_sem.at[i])

    def awaited(s, q, part):
        sent = (q != place) if s == 0 else (q > place)
        if part == 0:
            return sent
        passed = jnp.logical_and(lax.rem(q, 2) == lax.rem(place, 2), q > place)
        return jnp.logical_and(jnp.logical_not(passed), sent)

    def needed_parts(index):
        return (block_id(index) * KEEP + part_rows - 1) // part_rows

    lower_spans = needed_parts(per_span - 1) * (part_rows // half)

    def await_spans(s, low, high):
        for q in range(shards):
            wanted = jnp.logical_and(q >= low, q < high)

            for part in range(2):

                @pl.when(jnp.logical_and(wanted, awaited(s, q, part)))
                def _():
                    arrive(s, q, part)

    pass_on(1)

    handed = [
        pltpu.make_async_copy(source, target, hand_sem.at[n])
        for n, (source, target) in enumerate(
            [
                (qc.at[pl.ds(per_span, per_span)], qc_hbm),
                (kvc.at[pl.ds(per_span, per_span)], kvc_hbm),
                (gath, gath_hbm),
            ]
        )
    ]
    handed[0].start()
    handed[1].start()

    await_spans(0, 0, lower_spans)

    count = 2 - per_span % 2

    def step(n):
        index = n * count

        @pl.when(n == per_span // count - 1)
        def _():
            await_spans(0, lower_spans, shards)
            await_spans(1, 0, shards)
            handed[2].start()

        most = FAR_PARTS // 2
        attend_blocks(
            qc, kvc, gath, gain, out, index, count, block_id(index), part_rows, 1, most
        )
        for k in range(count):
            low_copy(index + k).start()

    loop(0, per_span // count, step)
    loop(0, per_span, lambda index: low_copy(index).wait())
    for copy in handed:
        copy.wait()

    for n in range(2):

        @pl.when(jnp.logical_not(last))
        def _():
            halo_copy(n, 0, 1).wait_send()

        @pl.when(jnp.logical_not(first))
        def _():
            halo_copy(n, 1, -1).wait_send()

    for part in range(2):
        own_copies(part, lambda copy: copy.wait_send())
    for d in range(1, chips):
        passed_copies(1, d, lambda copy: copy.wait_send())


def upper_kernel(
    shards,
    per_span,
    heads,
    low_hbm,
    qc_hbm,
    kvc_hbm,
    gath_hbm,
    gain_hbm,
    out_hbm,
    qc,
    kvc,
    gath,
    gain,
    out,
    low,
    in_sem,
    q_sem,
    out_sem,
    low_sem,
):
    place = lax.axis_index("ctx")
    block = TRANSFORM_BLOCK
    span_rows = per_span * block
    part_rows = 2 * shards * per_span * KEEP // FAR_PARTS

    loads = [
        pltpu.make_async_copy(source, target, in_sem.at[n])
        for n, (source, target) in enumerate(
            [(gath_hbm, gath), (kvc_hbm, kvc), (gain_hbm, gain)]
        )
    ]

    def query_load(i):
        return pltpu.make_async_copy(qc_hbm.at[i], qc.at[i], q_sem.at[i])

    query_load(0).start()
    for copy in loads:
        copy.start()
    loop(1, per_span, lambda i: query_load(i).start())
    low_load = pltpu.make_async_copy(low_hbm, low, low_sem.at[0])
    low_store = pltpu.make_async_copy(
        low, out_hbm.at[pl.ds(0, span_rows), :], low_sem.at[1]
    )
    low_load.start()

    def out_copy(i):
        rows = pl.ds(pl.multiple_of(i * block, block), block)
        target = pl.ds(pl.multiple_of(span_rows + i * block, block), block)
        return pltpu.make_async_copy(
            out.at[rows, :], out_hbm.at[target, :], out_sem.at[i]
        )

    for copy in loads:
        copy.wait()

    count = 2 - per_span % 2

    def step(n):
        i = n * count
        for k in range(count):
            query_load(i + k).wait()
        block_id = block_of(place, shards, per_span, per_span + i)
        least = FAR_PARTS // 2
        attend_blocks(
            qc, kvc, gath, gain, out, i, count, block_id, part_rows, least, FAR_PARTS
        )
        for k in range(count):
            out_copy(i + k).start()

        @pl.when(n == 0)
        def _():
            low_load.wait()
            low_store.start()

    loop(0, per_span // count, step)
    loop(0, per_span, lambda i: out_copy(i).wait())
    low_store.wait()


def attention(queries, pairs, query_taps, pair_taps, out_gain, shards):
    rows, columns = queries.shape
    span_rows = rows // 2
    per_span = span_rows // TRANSFORM_BLOCK
    heads = columns // HEAD_CHANNELS
    half = per_span * KEEP
    blocks = 2 * per_span
    bf16, f32 = jnp.bfloat16, jnp.float32
    width = 2 * HEAD_CHANNELS
    hbm = pl.BlockSpec(memory_space=pltpu.HBM)
    dma = pltpu.SemaphoreType.DMA
    gain = out_gain.reshape(1, columns)
    half_q = (per_span, heads, TRANSFORM_BLOCK, HEAD_CHANNELS)
    half_kv = (per_span, TRANSFORM_BLOCK, width)
    all_packed = (2 * shards, half, width)
    handed = pl.pallas_call(
        functools.partial(kernel, shards, per_span, heads),
        out_shape=[
            jax.ShapeDtypeStruct((span_rows, columns), bf16),
            jax.ShapeDtypeStruct(half_q, bf16),
            jax.ShapeDtypeStruct(half_kv, bf16),
            jax.ShapeDtypeStruct(all_packed, bf16),
        ],
        in_specs=[hbm] * 6,
        out_specs=[hbm] * 4,
        scratch_shapes=[
            pltpu.VMEM((2, HALO + span_rows, columns), bf16),
            pltpu.VMEM((2, HALO + span_rows, width), bf16),
            pltpu.VMEM((TAPS, columns), f32),
            pltpu.VMEM((TAPS, width), f32),
            pltpu.VMEM((1, columns), f32),
            pltpu.VMEM((KEEP, TRANSFORM_BLOCK), bf16),
            pltpu.VMEM((blocks, heads, TRANSFORM_BLOCK, HEAD_CHANNELS), bf16),
            pltpu.VMEM((blocks, TRANSFORM_BLOCK, width), bf16),
            pltpu.VMEM(all_packed, bf16),
            pltpu.VMEM((span_rows, columns), bf16),
            dma((4,)),
            dma((4,)),
            dma((2,)),
            dma((2, 2)),
            dma((2, 2)),
            dma((2, 2, 2 * shards)),
            dma((2, 2 * shards)),
            dma((per_span,)),
            dma((3,)),
        ],
        compiler_params=pltpu.CompilerParams(
            collective_id=0, has_side_effects=True, vmem_limit_bytes=62 * 1024 * 1024
        ),
        name="exchange_and_lower",
    )(
        queries,
        pairs,
        query_taps,
        pair_taps,
        gain,
        jnp.asarray(dct_table()),
    )
    return pl.pallas_call(
        functools.partial(upper_kernel, shards, per_span, heads),
        out_shape=jax.ShapeDtypeStruct((rows, columns), bf16),
        in_specs=[hbm] * 5,
        out_specs=hbm,
        scratch_shapes=[
            pltpu.VMEM(half_q, bf16),
            pltpu.VMEM(half_kv, bf16),
            pltpu.VMEM(all_packed, bf16),
            pltpu.VMEM((1, columns), f32),
            pltpu.VMEM((span_rows, columns), bf16),
            pltpu.VMEM((span_rows, columns), bf16),
            dma((3,)),
            dma((per_span,)),
            dma((per_span,)),
            dma((2,)),
        ],
        compiler_params=pltpu.CompilerParams(vmem_limit_bytes=62 * 1024 * 1024),
        name="upper",
    )(*handed, gain)


def from_partner(block, axis, apart):
    count = lax.axis_size(axis)
    route = []
    for low in range(count):
        high = low | 1 << apart
        if high != low and high < count:
            route += [(low, high), (high, low)]
    return lax.ppermute(block, axis, route)


def per_device(queries, keys_values, query_taps, pair_taps, out_gain):
    member = lax.axis_index("mp")
    width = keys_values.shape[1]
    rounds = (2 * HEAD_CHANNELS // width).bit_length() - 1

    def join(mine, bit):
        other = from_partner(mine, "mp", bit)
        lower = member // 2**bit % 2 == 0
        return jnp.where(
            lower, jnp.concatenate([mine, other], 1), jnp.concatenate([other, mine], 1)
        )

    for bit in range(rounds):
        keys_values = join(keys_values, bit)
        pair_taps = join(pair_taps, bit)
    return attention(
        queries, keys_values, query_taps, pair_taps, out_gain, lax.axis_size("ctx")
    )


def solution(mesh):
    in_specs = (P("ctx", "mp"), P("ctx", "mp"), P(None, "mp"), P(None, "mp"), P("mp"))
    out_specs = P("ctx", "mp")
    return jax.shard_map(
        per_device, mesh=mesh, in_specs=in_specs, out_specs=out_specs, check_vma=False
    )
```
